256 devices in a mesh: group: 8 (over x, core), dp: 32 (over y, z).
Axes of the slice: x: 4, y: 4, z: 8, core: 2. Of those that a mesh axis runs over, the one named last changes fastest.
Arguments:
- latent_cache: bfloat16 [1024, 384, 512], P(('group', 'dp')), parts along dimension 0, may hold values from -17 to 17
- rope_cache: bfloat16 [1024, 64, 384], P(('group', 'dp')), parts along dimension 0, may hold values from -6 to 6
- q_latent: bfloat16 [8, 1024, 128, 512], P(None, ('group', 'dp')), parts along dimension 1, may hold values from -16 to 16
- q_rope: bfloat16 [8, 1024, 64, 128], P(None, ('group', 'dp')), parts along dimension 1, may hold values from -6 to 6
- new_latent: bfloat16 [8, 1024, 512], P(None, ('group', 'dp')), parts along dimension 1, may hold values from -6 to 6
- new_rope: bfloat16 [8, 1024, 64], P(None, ('group', 'dp')), parts along dimension 1, may hold values from -6 to 6
- req_length: int32 [1024], P('group'), parts along dimension 0, may hold values from 16 to 376, as said below
- req_dest: int32 [1024], P('group'), parts along dimension 0, may hold values from 0 to 31, as said below
Outputs:
- attention: bfloat16 [8, 1024, 128, 512], P(None, ('group', 'dp')), parts along dimension 1
- moved_latent: bfloat16 [1024, 384, 512], P(('group', 'dp')), parts along dimension 0
- moved_rope: bfloat16 [1024, 64, 384], P(('group', 'dp')), parts along dimension 0
The draws below stay inside these ranges and needn't reach their ends.
There are 8 independent parts, one for each index of `group`. The reference program is written for one: setup_inputs(seed, part) draws one part's arguments, and reference() takes and returns one part's arrays. A program takes and returns all parts, laid end to end along the dimension named above; each array names one. Nothing has to cross between parts.
Inputs may be any that keep to these rules, and one draw needn't show every extreme that they name: Request r starts on rank r // 4 in slot r % 4 and goes to slot r % 4 of rank req_dest[r]. Every move is a swap of that slot between two ranks, so each rank holds 4 requests after the move; at most one request goes from one rank to another one, and in every draw some rank receives 4 requests from others. `req_length`: in every draw some request has exactly 376 cached tokens.
All inputs are finite; a program needn't handle non-finite values.
Results may differ from the reference program's by a relative error of at most 0.0048.
Values may be sent and summed in bfloat16 or wider, within the bound.
A program may use at most 128 MiB of HBM per device.

```python
import jax
import jax.numpy as jnp
from jax import lax

DL = 512
DR = 64
HEADS = 128
REQ_DEV = 4
LMAX = 384
STEPS = 8
MINLEN = 16
NREQ = 128
N_DP = 32


def draw_latent_cache(key, part):
    key = jax.random.fold_in(key, 31)
    key_one = jax.random.fold_in(key, 0)
    shape = (NREQ, LMAX, DL)
    values = jnp.clip(jax.random.normal(key_one, shape), -6.0, 6.0)
    return values.astype(jnp.bfloat16)


def draw_q_latent(key, part):
    key = jax.random.fold_in(key, 32)
    key_one = jax.random.fold_in(key, 0)
    shape = (STEPS, NREQ, HEADS, DL)
    values = jnp.clip(jax.random.normal(key_one, shape), -6.0, 6.0)
    return values.astype(jnp.bfloat16)


def draw_req_length(key, part):
    key = jax.random.fold_in(key, 33)
    key_one, key_two = jax.random.split(key, 2)
    cube_root = jax.random.randint(key_one, (NREQ,), 0, 9)
    length_span = LMAX - STEPS - MINLEN
    lengths = LMAX - STEPS - length_span * cube_root * cube_root * cube_root // 512
    longest = jax.random.randint(key_two, (), 0, NREQ)
    lengths = jnp.where(jnp.arange(NREQ) == longest, LMAX - STEPS, lengths)
    return lengths.astype(jnp.int32)


def draw_req_dest(key, part):
    key = jax.random.fold_in(key, 34)
    key_one, key_two = jax.random.split(key, 2)
    rank_label = jax.random.permutation(key_one, N_DP).astype(jnp.int32)
    rank_of = jnp.zeros((N_DP,), jnp.int32).at[rank_label].set(jnp.arange(N_DP, dtype=jnp.int32))
    xor_masks = (jax.random.permutation(key_two, N_DP - 1)[:REQ_DEV] + 1).astype(jnp.int32)
    partner_label = jnp.bitwise_xor(rank_label[:, None], xor_masks[None, :])
    partner = rank_of[partner_label]
    return partner.reshape(-1).astype(jnp.int32)


def block_levels(stream_key, dims, pieces, smallest, largest):
    factor_of = 1.0
    for axis_at, blocks in pieces:
        steps = jax.random.uniform(jax.random.fold_in(jax.random.fold_in(stream_key, 6), axis_at), (blocks,), jnp.float32, smallest / len(pieces), largest / len(pieces))
        factor_of = factor_of * jnp.repeat(jnp.exp(steps), dims[axis_at] // blocks).reshape((-1,) + (1,) * (len(dims) - 1 - axis_at))
    return factor_of


def normal_values(stream_key, dims, spread, reach, pieces=(), kind=jnp.bfloat16):
    drawn = jax.random.normal(stream_key, dims, jnp.float32) * spread
    if len(pieces) > 0:
        drawn = block_levels(stream_key, dims, pieces, -0.22, 0.18) * drawn
    return jnp.clip(drawn, min=-reach, max=reach).astype(kind)


def setup_inputs(seed: int = 0, part: int = 0) -> dict:
    seeds = jax.random.split(jax.random.key(seed), 9)
    own_keys = jax.random.split(jax.random.fold_in(seeds[8], part), 9)
    latent_cache = draw_latent_cache(jax.random.fold_in(jax.random.fold_in(seeds[8], part), 71), part)
    rope_cache = normal_values(own_keys[1], (NREQ, DR, LMAX), 1.0, 6.0, ((0, 32),))
    q_latent = draw_q_latent(jax.random.fold_in(jax.random.fold_in(seeds[8], part), 71), part)
    q_rope = normal_values(own_keys[3], (STEPS, NREQ, DR, HEADS), 1.0, 6.0, ((1, 32),))
    new_latent = normal_values(own_keys[4], (STEPS, NREQ, DL), 1.0, 6.0, ((1, 32),))
    new_rope = normal_values(own_keys[5], (STEPS, NREQ, DR), 1.0, 6.0, ((1, 32),))
    req_length = draw_req_length(jax.random.fold_in(jax.random.fold_in(seeds[8], part), 71), part)
    req_dest = draw_req_dest(jax.random.fold_in(jax.random.fold_in(seeds[8], part), 71), part)
    return {"latent_cache": latent_cache, "rope_cache": rope_cache, "q_latent": q_latent, "q_rope": q_rope, "new_latent": new_latent, "new_rope": new_rope, "req_length": req_length, "req_dest": req_dest}


SCORE_SCALE = 192.0 ** -0.5


def reference(latent_cache, rope_cache, q_latent, q_rope, new_latent, new_rope, req_length, req_dest):
    request_ids = jnp.arange(N_DP * REQ_DEV, dtype=jnp.int32)
    after_slot = (req_dest * REQ_DEV + request_ids % REQ_DEV).astype(jnp.int32)
    source_of = jnp.zeros((N_DP * REQ_DEV,), jnp.int32).at[after_slot].set(request_ids)
    positions = jnp.arange(LMAX, dtype=jnp.int32)
    step_ids = jnp.arange(STEPS, dtype=jnp.int32)

    def per_slot(slot_index):
        request = source_of[slot_index]
        length = req_length[request]
        offsets = positions - length
        picked = jnp.clip(offsets, 0, STEPS - 1).astype(jnp.int32)
        fresh_latent = new_latent[:, slot_index][picked]
        fresh_rope = jnp.transpose(new_rope[:, slot_index][picked])
        resident = offsets < 0
        written = offsets < STEPS
        moved_lat = jnp.where(resident[:, None], latent_cache[request],
                              jnp.where(written[:, None], fresh_latent, jnp.zeros_like(fresh_latent)))
        moved_rot = jnp.where(resident[None, :], rope_cache[request],
                              jnp.where(written[None, :], fresh_rope, jnp.zeros_like(fresh_rope)))
        scores = (jnp.einsum("thc,lc->thl", q_latent[:, slot_index].astype(jnp.float32), moved_lat.astype(jnp.float32))
                  + jnp.einsum("tch,cl->thl", q_rope[:, slot_index].astype(jnp.float32), moved_rot.astype(jnp.float32))) * SCORE_SCALE
        visible = positions[None, :] < length + step_ids[:, None] + 1
        scores = jnp.where(visible[:, None, :], scores, -jnp.inf)
        row_max = jnp.max(scores, axis=-1, keepdims=True)
        raised = jnp.exp(scores - row_max)
        weights = (raised / jnp.sum(raised, axis=-1, keepdims=True)).astype(jnp.bfloat16)
        result = jnp.einsum("thl,lc->thc", weights.astype(jnp.float32), moved_lat.astype(jnp.float32)).astype(jnp.bfloat16)
        return result, moved_lat, moved_rot

    attention, moved_latent, moved_rope = lax.map(per_slot, request_ids)
    return jnp.transpose(attention, (1, 0, 2, 3)), moved_latent, moved_rope
```

```python
import math

import jax
import jax.numpy as jnp
from jax import lax
from jax.experimental import pallas as pl
from jax.experimental.pallas import tpu as pltpu
from jax.sharding import PartitionSpec as P

MESH = pl.DeviceIdType.MESH
RANKS = 32
RING = 8
SLOTS = 4
ROWS = 384
LATENT = 512
ROPE = 64
STEPS = 8
HEADS = 128
PIECE_ROWS = 48
TILE = 128
ROPE_UNITS = 12
LOG2E_SCALE = 192.0 ** (-0.5) * math.log2(math.e)


def shifted(rank, k):
    y, z = rank // RING, rank % RING
    return (y + k // RING) % 4 * RING + (z + 3 * k) % RING


def latent_piece(ref, slot, piece):
    row = pl.multiple_of(piece // 4 * PIECE_ROWS, PIECE_ROWS)
    column = pl.multiple_of(piece % 4 * TILE, TILE)
    return ref.at[slot, pl.ds(row, PIECE_ROWS), pl.ds(column, TILE)]


def rope_unit(ref, slot, unit):
    row = pl.multiple_of(unit % 4 * 16, 16)
    column = pl.multiple_of(unit // 4 * TILE, TILE)
    return ref.at[slot, pl.ds(row, 16), pl.ds(column, TILE)]


def exchange_kernel(
    dest_ref, latent_ref, rope_ref, out_latent, out_rope,
    held, staged, held_rope, staged_rope,
    send_one, recv_one, send_two, recv_two,
    send_one_rope, recv_one_rope, send_two_rope, recv_two_rope,
):
    me = lax.axis_index("dp")
    barrier = pltpu.get_barrier_semaphore()

    @pl.loop(1, RANKS)
    def _(k):
        pl.semaphore_signal(barrier, inc=1, device_id={"dp": shifted(me, k)}, device_id_type=MESH)

    pl.semaphore_wait(barrier, RANKS - 1)

    def rope_slot_of(u):
        return (me + RANKS * u) // ROPE_UNITS

    def send_rope(slot):
        @pl.loop(0, ROPE_UNITS)
        def _(i):
            q = (i + me) % ROPE_UNITS
            unit = slot * ROPE_UNITS + q
            peer, u = unit % RANKS, unit // RANKS
            source = rope_unit(rope_ref, slot, q)

            for w in range(2):
                if slot * ROPE_UNITS // RANKS <= w <= (slot * ROPE_UNITS + ROPE_UNITS - 1) // RANKS:
                    target = held_rope[w].at[me]

                    @pl.when((u == w) & (peer == me))
                    def _():
                        pltpu.make_async_copy(source, target, recv_one_rope.at[w]).start()

                    @pl.when((u == w) & (peer != me))
                    def _():
                        pltpu.make_async_remote_copy(
                            source, target, send_one_rope.at[slot], recv_one_rope.at[w],
                            device_id={"dp": peer}, device_id_type=MESH,
                        ).start()

    for slot in range(SLOTS):
        pltpu.make_async_copy(
            latent_piece(latent_ref, slot, me), held[slot].at[me], recv_one.at[slot]
        ).start()

        @pl.loop(1, RANKS)
        def _(k):
            peer = shifted(me, k)
            pltpu.make_async_remote_copy(
                latent_piece(latent_ref, slot, peer), held[slot].at[me],
                send_one.at[slot], recv_one.at[slot],
                device_id={"dp": peer}, device_id_type=MESH,
            ).start()

        send_rope(slot)

    def forward_rope(u):
        pltpu.make_async_copy(held_rope[u], held_rope[u], recv_one_rope.at[u]).wait()
        unit = me + RANKS * u
        slot, q = unit // ROPE_UNITS, unit % ROPE_UNITS

        @pl.loop(0, RANKS)
        def _(k):
            peer = shifted(me, k)
            origin = dest_ref[peer * SLOTS + slot]
            staged_rope[u, peer] = held_rope[u][origin]
            source, target = staged_rope.at[u, peer], rope_unit(out_rope, slot, q)

            @pl.when(k == 0)
            def _():
                pltpu.make_async_copy(source, target, recv_two_rope.at[slot]).start()

            @pl.when(k != 0)
            def _():
                pltpu.make_async_remote_copy(
                    source, target, send_two_rope.at[u], recv_two_rope.at[slot],
                    device_id={"dp": peer}, device_id_type=MESH,
                ).start()

    for slot in range(SLOTS):
        pltpu.make_async_copy(held[slot], held[slot], recv_one.at[slot]).wait()

        @pl.loop(0, RANKS)
        def _(k):
            peer = shifted(me, k)
            origin = dest_ref[peer * SLOTS + slot]
            staged[slot, peer] = held[slot][origin]
            source, target = staged.at[slot, peer], latent_piece(out_latent, slot, me)

            @pl.when(k == 0)
            def _():
                pltpu.make_async_copy(source, target, recv_two.at[slot]).start()

            @pl.when(k != 0)
            def _():
                pltpu.make_async_remote_copy(
                    source, target, send_two.at[slot], recv_two.at[slot],
                    device_id={"dp": peer}, device_id_type=MESH,
                ).start()

        if slot == 2:
            forward_rope(0)
        if slot == 3:
            pl.when(me < 16)(lambda: forward_rope(1))

    for slot in range(SLOTS):
        pltpu.make_async_copy(out_latent.at[slot], out_latent.at[slot], recv_two.at[slot]).wait()
        pltpu.make_async_copy(out_rope.at[slot], out_rope.at[slot], recv_two_rope.at[slot]).wait()

    others = pl.ds(0, RANKS - 1)
    for slot in range(SLOTS):
        pltpu.make_async_copy(held[slot].at[others], held[slot].at[others], send_one.at[slot]).wait()
        pltpu.make_async_copy(staged.at[slot, others], staged.at[slot, others], send_two.at[slot]).wait()
        own = (rope_slot_of(0) == slot) | ((me < 16) & (rope_slot_of(1) == slot))

        @pl.when(own)
        def _():
            part = held_rope[0].at[pl.ds(0, ROPE_UNITS - 1)]
            pltpu.make_async_copy(part, part, send_one_rope.at[slot]).wait()

        @pl.when(jnp.logical_not(own))
        def _():
            part = held_rope[0].at[pl.ds(0, ROPE_UNITS)]
            pltpu.make_async_copy(part, part, send_one_rope.at[slot]).wait()

    rest = staged_rope.at[0, pl.ds(0, RANKS - 1)]
    pltpu.make_async_copy(rest, rest, send_two_rope.at[0]).wait()

    @pl.when(me < 16)
    def _():
        pltpu.make_async_copy(rest, rest, send_two_rope.at[1]).wait()


def exchange(req_dest, latent_cache, rope_cache):
    anywhere = pl.BlockSpec(memory_space=pl.ANY)
    dma = pltpu.SemaphoreType.DMA
    return pl.pallas_call(
        exchange_kernel,
        out_shape=(
            jax.ShapeDtypeStruct(latent_cache.shape, jnp.bfloat16),
            jax.ShapeDtypeStruct(rope_cache.shape, jnp.bfloat16),
        ),
        in_specs=[pl.BlockSpec(memory_space=pltpu.SMEM), anywhere, anywhere],
        out_specs=(anywhere, anywhere),
        scratch_shapes=[
            (pltpu.VMEM((RANKS, PIECE_ROWS, TILE), jnp.bfloat16),) * SLOTS,
            pltpu.VMEM((SLOTS, RANKS, PIECE_ROWS, TILE), jnp.bfloat16),
            (pltpu.VMEM((RANKS, 16, TILE), jnp.bfloat16),) * 2,
            pltpu.VMEM((2, RANKS, 16, TILE), jnp.bfloat16),
            dma((SLOTS,)), dma((SLOTS,)), dma((SLOTS,)), dma((SLOTS,)),
            dma((SLOTS,)), dma((2,)), dma((2,)), dma((SLOTS,)),
        ],
        compiler_params=pltpu.CompilerParams(
            collective_id=0, has_side_effects=True, vmem_limit_bytes=16 * 2**20
        ),
        cost_estimate=pl.CostEstimate(flops=0, bytes_accessed=8 * 2**20, transcendentals=0),
        name="exchange",
    )(req_dest, latent_cache, rope_cache)


def attend_kernel(
    dest_ref, length_ref, latent_ref, rope_ref, q_ref, q_rope_ref, new_ref, new_rope_ref,
    out_ref, moved_ref, moved_rope_ref, fresh, fresh_rope,
):
    me = lax.axis_index("dp")
    slot = pl.program_id(0)
    length = length_ref[dest_ref[me * SLOTS + slot] * SLOTS + slot]

    for k in range(SLOTS):
        @pl.when(slot == k)
        def _():
            fresh[...] = new_ref[:, k, :]
            fresh_rope[...] = new_rope_ref[:, k, :]

    row = lax.broadcasted_iota(jnp.int32, (ROWS, STEPS), 0)
    step = lax.broadcasted_iota(jnp.int32, (ROWS, STEPS), 1)
    placed = jnp.where(row - length == step, 1.0, 0.0).astype(jnp.bfloat16)
    added = jnp.dot(placed, fresh[...], preferred_element_type=jnp.float32).astype(jnp.bfloat16)
    position = lax.broadcasted_iota(jnp.int32, (ROWS, LATENT), 0)
    keys = jnp.where(position < length, latent_ref[0], added)
    moved_ref[0] = keys

    added_rope = lax.dot_general(
        fresh_rope[...], placed, (((0,), (1,)), ((), ())), preferred_element_type=jnp.float32
    ).astype(jnp.bfloat16)
    position = lax.broadcasted_iota(jnp.int32, (ROPE, ROWS), 1)
    keys_rope = jnp.where(position < length, rope_ref[0], added_rope)
    moved_rope_ref[0] = keys_rope

    column = lax.broadcasted_iota(jnp.int32, (HEADS, ROWS), 1)
    for t in range(STEPS):
        scores = lax.dot_general(
            q_ref[t, 0], keys, (((1,), (1,)), ((), ())), preferred_element_type=jnp.float32
        ) + lax.dot_general(
            q_rope_ref[t, 0], keys_rope, (((0,), (0,)), ((), ())), preferred_element_type=jnp.float32
        )
        scores = jnp.where(column <= length + t, scores * LOG2E_SCALE, -jnp.inf)
        raised = jnp.exp2(scores - jnp.max(scores, axis=1, keepdims=True))
        total = jnp.sum(raised, axis=1, keepdims=True)
        result = jnp.dot(raised.astype(jnp.bfloat16), keys, preferred_element_type=jnp.float32)
        out_ref[t, 0] = (result * (1.0 / total)).astype(jnp.bfloat16)


def attend(req_dest, req_length, latent, rope, q_latent, q_rope, new_latent, new_rope):
    scalars = pl.BlockSpec(memory_space=pltpu.SMEM)
    by_slot = lambda *shape: pl.BlockSpec((1, *shape), lambda j: (j, 0, 0))
    by_step = lambda *shape: pl.BlockSpec((STEPS, 1, *shape), lambda j: (0, j, 0, 0))
    whole = lambda array: pl.BlockSpec(array.shape, lambda j: (0, 0, 0))
    return pl.pallas_call(
        attend_kernel,
        grid=(SLOTS,),
        out_shape=(
            jax.ShapeDtypeStruct(q_latent.shape, jnp.bfloat16),
            jax.ShapeDtypeStruct(latent.shape, jnp.bfloat16),
            jax.ShapeDtypeStruct(rope.shape, jnp.bfloat16),
        ),
        in_specs=[
            scalars, scalars, by_slot(ROWS, LATENT), by_slot(ROPE, ROWS),
            by_step(HEADS, LATENT), by_step(ROPE, HEADS), whole(new_latent), whole(new_rope),
        ],
        out_specs=(by_step(HEADS, LATENT), by_slot(ROWS, LATENT), by_slot(ROPE, ROWS)),
        scratch_shapes=[
            pltpu.VMEM((STEPS, LATENT), jnp.bfloat16),
            pltpu.VMEM((STEPS, ROPE), jnp.bfloat16),
        ],
        compiler_params=pltpu.CompilerParams(vmem_limit_bytes=32 * 2**20),
        cost_estimate=pl.CostEstimate(
            flops=3_500_000_000, bytes_accessed=12 * 2**20, transcendentals=1_600_000
        ),
        name="attend",
    )(req_dest, req_length, latent, rope, q_latent, q_rope, new_latent, new_rope)


def body(latent_cache, rope_cache, q_latent, q_rope, new_latent, new_rope, req_length, req_dest):
    latent, rope = exchange(req_dest, latent_cache, rope_cache)
    return attend(req_dest, req_length, latent, rope, q_latent, q_rope, new_latent, new_rope)


def solution(mesh):
    return jax.shard_map(
        body,
        mesh=mesh,
        in_specs=(
            P(("group", "dp"), None, None),
            P(("group", "dp"), None, None),
            P(None, ("group", "dp"), None, None),
            P(None, ("group", "dp"), None, None),
            P(None, ("group", "dp"), None),
            P(None, ("group", "dp"), None),
            P("group"),
            P("group"),
        ),
        out_specs=(
            P(None, ("group", "dp"), None, None),
            P(("group", "dp"), None, None),
            P(("group", "dp"), None, None),
        ),
        check_vma=False,
    )
```

```python
import math

import jax
import jax.numpy as jnp
from jax import lax
from jax.experimental import pallas as pl
from jax.experimental.pallas import tpu as pltpu
from jax.sharding import PartitionSpec as P

MESH = pl.DeviceIdType.MESH
RANKS = 32
RING = 8
SLOTS = 4
ROWS = 384
LATENT = 512
ROPE = 64
STEPS = 8
HEADS = 128
PIECE_ROWS = 48
TILE = 128
ROPE_UNITS = 12
LOG2E_SCALE = 192.0 ** (-0.5) * math.log2(math.e)


def shifted(rank, k):
    y, z = rank // RING, rank % RING
    return (y + k // RING) % 4 * RING + (z + 3 * k) % RING


def latent_piece(ref, slot, piece):
    row = pl.multiple_of(piece // 4 * PIECE_ROWS, PIECE_ROWS)
    column = pl.multiple_of(piece % 4 * TILE, TILE)
    return ref.at[slot, pl.ds(row, PIECE_ROWS), pl.ds(column, TILE)]


def rope_unit(ref, slot, unit):
    row = pl.multiple_of(unit % 4 * 16, 16)
    column = pl.multiple_of(unit // 4 * TILE, TILE)
    return ref.at[slot, pl.ds(row, 16), pl.ds(column, TILE)]


def exchange_kernel(
    dest_ref, latent_ref, rope_ref, out_latent, out_rope,
    held, staged, held_rope, staged_rope,
    send_one, recv_one, send_two, recv_two,
    send_one_rope, recv_one_rope, send_two_rope, recv_two_rope,
):
    me = lax.axis_index("dp")
    barrier = pltpu.get_barrier_semaphore()

    @pl.loop(1, RANKS)
    def _(k):
        pl.semaphore_signal(barrier, inc=1, device_id={"dp": shifted(me, k)}, device_id_type=MESH)

    pl.semaphore_wait(barrier, RANKS - 1)

    def rope_slot_of(u):
        return (me + RANKS * u) // ROPE_UNITS

    def send_rope(slot):
        @pl.loop(0, ROPE_UNITS)
        def _(i):
            q = (i + me) % ROPE_UNITS
            unit = slot * ROPE_UNITS + q
            peer, u = unit % RANKS, unit // RANKS
            source = rope_unit(rope_ref, slot, q)

            for w in range(2):
                if slot * ROPE_UNITS // RANKS <= w <= (slot * ROPE_UNITS + ROPE_UNITS - 1) // RANKS:
                    target = held_rope[w].at[me]

                    @pl.when((u == w) & (peer == me))
                    def _():
                        pltpu.make_async_copy(source, target, recv_one_rope.at[w]).start()

                    @pl.when((u == w) & (peer != me))
                    def _():
                        pltpu.make_async_remote_copy(
                            source, target, send_one_rope.at[slot], recv_one_rope.at[w],
                            device_id={"dp": peer}, device_id_type=MESH,
                        ).start()

    for slot in range(SLOTS):
        pltpu.make_async_copy(
            latent_piece(latent_ref, slot, me), held[slot].at[me], recv_one.at[slot]
        ).start()

        @pl.loop(1, RANKS)
        def _(k):
            peer = shifted(me, k)
            pltpu.make_async_remote_copy(
                latent_piece(latent_ref, slot, peer), held[slot].at[me],
                send_one.at[slot], recv_one.at[slot],
                device_id={"dp": peer}, device_id_type=MESH,
            ).start()

        send_rope(slot)

    def forward_rope(u):
        pltpu.make_async_copy(held_rope[u], held_rope[u], recv_one_rope.at[u]).wait()
        unit = me + RANKS * u
        slot, q = unit // ROPE_UNITS, unit % ROPE_UNITS

        @pl.loop(0, RANKS)
        def _(k):
            peer = shifted(me, k)
            origin = dest_ref[peer * SLOTS + slot]
            staged_rope[u, peer] = held_rope[u][origin]
            source, target = staged_rope.at[u, peer], rope_unit(out_rope, slot, q)

            @pl.when(k == 0)
            def _():
                pltpu.make_async_copy(source, target, recv_two_rope.at[slot]).start()

            @pl.when(k != 0)
            def _():
                pltpu.make_async_remote_copy(
                    source, target, send_two_rope.at[u], recv_two_rope.at[slot],
                    device_id={"dp": peer}, device_id_type=MESH,
                ).start()

    for slot in range(SLOTS):
        pltpu.make_async_copy(held[slot], held[slot], recv_one.at[slot]).wait()

        @pl.loop(0, RANKS)
        def _(k):
            peer = shifted(me, k)
            origin = dest_ref[peer * SLOTS + slot]
            staged[slot, peer] = held[slot][origin]
            source, target = staged.at[slot, peer], latent_piece(out_latent, slot, me)

            @pl.when(k == 0)
            def _():
                pltpu.make_async_copy(source, target, recv_two.at[slot]).start()

            @pl.when(k != 0)
            def _():
                pltpu.make_async_remote_copy(
                    source, target, send_two.at[slot], recv_two.at[slot],
                    device_id={"dp": peer}, device_id_type=MESH,
                ).start()

        if slot == 2:
            forward_rope(0)
        if slot == 3:
            pl.when(me < 16)(lambda: forward_rope(1))

    for slot in range(SLOTS):
        pltpu.make_async_copy(out_latent.at[slot], out_latent.at[slot], recv_two.at[slot]).wait()
        pltpu.make_async_copy(out_rope.at[slot], out_rope.at[slot], recv_two_rope.at[slot]).wait()

    others = pl.ds(0, RANKS - 1)
    for slot in range(SLOTS):
        pltpu.make_async_copy(held[slot].at[others], held[slot].at[others], send_one.at[slot]).wait()
        pltpu.make_async_copy(staged.at[slot, others], staged.at[slot, others], send_two.at[slot]).wait()
        own = (rope_slot_of(0) == slot) | ((me < 16) & (rope_slot_of(1) == slot))

        @pl.when(own)
        def _():
            part = held_rope[0].at[pl.ds(0, ROPE_UNITS - 1)]
            pltpu.make_async_copy(part, part, send_one_rope.at[slot]).wait()

        @pl.when(jnp.logical_not(own))
        def _():
            part = held_rope[0].at[pl.ds(0, ROPE_UNITS)]
            pltpu.make_async_copy(part, part, send_one_rope.at[slot]).wait()

    rest = staged_rope.at[0, pl.ds(0, RANKS - 1)]
    pltpu.make_async_copy(rest, rest, send_two_rope.at[0]).wait()

    @pl.when(me < 16)
    def _():
        pltpu.make_async_copy(rest, rest, send_two_rope.at[1]).wait()


def exchange(req_dest, latent_cache, rope_cache):
    anywhere = pl.BlockSpec(memory_space=pl.ANY)
    dma = pltpu.SemaphoreType.DMA
    return pl.pallas_call(
        exchange_kernel,
        out_shape=(
            jax.ShapeDtypeStruct(latent_cache.shape, jnp.bfloat16),
            jax.ShapeDtypeStruct(rope_cache.shape, jnp.bfloat16),
        ),
        in_specs=[pl.BlockSpec(memory_space=pltpu.SMEM), anywhere, anywhere],
        out_specs=(anywhere, anywhere),
        scratch_shapes=[
            (pltpu.VMEM((RANKS, PIECE_ROWS, TILE), jnp.bfloat16),) * SLOTS,
            pltpu.VMEM((SLOTS, RANKS, PIECE_ROWS, TILE), jnp.bfloat16),
            (pltpu.VMEM((RANKS, 16, TILE), jnp.bfloat16),) * 2,
            pltpu.VMEM((2, RANKS, 16, TILE), jnp.bfloat16),
            dma((SLOTS,)), dma((SLOTS,)), dma((SLOTS,)), dma((SLOTS,)),
            dma((SLOTS,)), dma((2,)), dma((2,)), dma((SLOTS,)),
        ],
        compiler_params=pltpu.CompilerParams(
            collective_id=0, has_side_effects=True, vmem_limit_bytes=60 * 2**20
        ),
        cost_estimate=pl.CostEstimate(flops=0, bytes_accessed=8 * 2**20, transcendentals=0),
        name="exchange",
    )(req_dest, latent_cache, rope_cache)


def attend_kernel(
    dest_ref, length_ref, latent_ref, rope_ref, q_ref, q_rope_ref, new_ref, new_rope_ref,
    out_ref, moved_ref, moved_rope_ref, fresh, fresh_rope,
):
    me = lax.axis_index("dp")
    slot = pl.program_id(0)
    length = length_ref[dest_ref[me * SLOTS + slot] * SLOTS + slot]

    for k in range(SLOTS):
        @pl.when(slot == k)
        def _():
            fresh[...] = new_ref[:, k, :]
            fresh_rope[...] = new_rope_ref[:, k, :]

    row = lax.broadcasted_iota(jnp.int32, (ROWS, STEPS), 0)
    step = lax.broadcasted_iota(jnp.int32, (ROWS, STEPS), 1)
    placed = jnp.where(row - length == step, 1.0, 0.0).astype(jnp.bfloat16)
    added = jnp.dot(placed, fresh[...], preferred_element_type=jnp.float32).astype(jnp.bfloat16)
    position = lax.broadcasted_iota(jnp.int32, (ROWS, LATENT), 0)
    keys = jnp.where(position < length, latent_ref[0], added)
    moved_ref[0] = keys

    added_rope = lax.dot_general(
        fresh_rope[...], placed, (((0,), (1,)), ((), ())), preferred_element_type=jnp.float32
    ).astype(jnp.bfloat16)
    position = lax.broadcasted_iota(jnp.int32, (ROPE, ROWS), 1)
    keys_rope = jnp.where(position < length, rope_ref[0], added_rope)
    moved_rope_ref[0] = keys_rope

    shape = (STEPS, HEADS, ROWS)
    seen = lax.broadcasted_iota(jnp.int32, shape, 2) <= length + lax.broadcasted_iota(jnp.int32, shape, 0)
    queries = q_ref[:, 0].reshape(STEPS * HEADS, LATENT)
    queries_rope = jnp.concatenate([q_rope_ref[t, 0].T for t in range(STEPS)], axis=0)
    scores = lax.dot_general(
        queries, moved_ref[0], (((1,), (1,)), ((), ())), preferred_element_type=jnp.float32
    ) + jnp.dot(queries_rope, moved_rope_ref[0], preferred_element_type=jnp.float32)
    scores = jnp.where(seen.reshape(STEPS * HEADS, ROWS), scores * LOG2E_SCALE, -jnp.inf)
    raised = jnp.exp2(scores - jnp.max(scores, axis=1, keepdims=True))
    total = jnp.sum(raised, axis=1, keepdims=True)
    result = jnp.dot(raised.astype(jnp.bfloat16), moved_ref[0], preferred_element_type=jnp.float32)
    out_ref[:, 0] = (result * (1.0 / total)).astype(jnp.bfloat16).reshape(STEPS, HEADS, LATENT)


def attend(req_dest, req_length, latent, rope, q_latent, q_rope, new_latent, new_rope):
    scalars = pl.BlockSpec(memory_space=pltpu.SMEM)
    by_slot = lambda *shape: pl.BlockSpec((1, *shape), lambda j: (j, 0, 0))
    by_step = lambda *shape: pl.BlockSpec((STEPS, 1, *shape), lambda j: (0, j, 0, 0))
    whole = lambda array: pl.BlockSpec(array.shape, lambda j: (0, 0, 0))
    return pl.pallas_call(
        attend_kernel,
        grid=(SLOTS,),
        out_shape=(
            jax.ShapeDtypeStruct(q_latent.shape, jnp.bfloat16),
            jax.ShapeDtypeStruct(latent.shape, jnp.bfloat16),
            jax.ShapeDtypeStruct(rope.shape, jnp.bfloat16),
        ),
        in_specs=[
            scalars, scalars, by_slot(ROWS, LATENT), by_slot(ROPE, ROWS),
            by_step(HEADS, LATENT), by_step(ROPE, HEADS), whole(new_latent), whole(new_rope),
        ],
        out_specs=(by_step(HEADS, LATENT), by_slot(ROWS, LATENT), by_slot(ROPE, ROWS)),
        scratch_shapes=[
            pltpu.VMEM((STEPS, LATENT), jnp.bfloat16),
            pltpu.VMEM((STEPS, ROPE), jnp.bfloat16),
        ],
        compiler_params=pltpu.CompilerParams(vmem_limit_bytes=60 * 2**20),
        cost_estimate=pl.CostEstimate(
            flops=3_500_000_000, bytes_accessed=12 * 2**20, transcendentals=1_600_000
        ),
        name="attend",
    )(req_dest, req_length, latent, rope, q_latent, q_rope, new_latent, new_rope)


def body(latent_cache, rope_cache, q_latent, q_rope, new_latent, new_rope, req_length, req_dest):
    latent, rope = exchange(req_dest, latent_cache, rope_cache)
    return attend(req_dest, req_length, latent, rope, q_latent, q_rope, new_latent, new_rope)


def solution(mesh):
    return jax.shard_map(
        body,
        mesh=mesh,
        in_specs=(
            P(("group", "dp"), None, None),
            P(("group", "dp"), None, None),
            P(None, ("group", "dp"), None, None),
            P(None, ("group", "dp"), None, None),
            P(None, ("group", "dp"), None),
            P(None, ("group", "dp"), None),
            P("group"),
            P("group"),
        ),
        out_specs=(
            P(None, ("group", "dp"), None, None),
            P(("group", "dp"), None, None),
            P(("group", "dp"), None, None),
        ),
        check_vma=False,
    )
```

```python
import math

import jax
import jax.numpy as jnp
from jax import lax
from jax.experimental import pallas as pl
from jax.experimental.pallas import tpu as pltpu
from jax.sharding import PartitionSpec as P

MESH = pl.DeviceIdType.MESH
RANKS = 32
RING = 8
SLOTS = 4
ROWS = 384
LATENT = 512
ROPE = 64
STEPS = 8
HEADS = 128
PIECE_ROWS = 48
TILE = 128
ROPE_UNITS = 12
EARLY = 3
LOG2E_SCALE = 192.0 ** (-0.5) * math.log2(math.e)


def shifted(rank, k):
    y, z = rank // RING, rank % RING
    return (y + k // RING) % 4 * RING + (z + 3 * k) % RING


def rope_place(rank):
    y, z = rank // RING, rank % RING
    return (y + z) % 2 * 16 + y * 4 + z // 2


def rope_rank(place):
    half, y, z = place // 16, place % 16 // 4, place % 4
    return y * RING + 2 * z + (y + half) % 2


def latent_piece(ref, slot, piece):
    row = pl.multiple_of(piece // 4 * PIECE_ROWS, PIECE_ROWS)
    column = pl.multiple_of(piece % 4 * TILE, TILE)
    return ref.at[slot, pl.ds(row, PIECE_ROWS), pl.ds(column, TILE)]


def rope_unit(ref, slot, unit):
    row = pl.multiple_of(unit % 4 * 16, 16)
    column = pl.multiple_of(unit // 4 * TILE, TILE)
    return ref.at[slot, pl.ds(row, 16), pl.ds(column, TILE)]


def merged(length, latent, rope, fresh, fresh_rope):
    row = lax.broadcasted_iota(jnp.int32, (ROWS, STEPS), 0)
    step = lax.broadcasted_iota(jnp.int32, (ROWS, STEPS), 1)
    placed = jnp.where(row - length == step, 1.0, 0.0).astype(jnp.bfloat16)
    added = jnp.dot(placed, fresh, preferred_element_type=jnp.float32).astype(jnp.bfloat16)
    position = lax.broadcasted_iota(jnp.int32, (ROWS, LATENT), 0)
    added_rope = lax.dot_general(
        fresh_rope, placed, (((0,), (1,)), ((), ())), preferred_element_type=jnp.float32
    ).astype(jnp.bfloat16)
    position_rope = lax.broadcasted_iota(jnp.int32, (ROPE, ROWS), 1)
    return (
        jnp.where(position < length, latent, added),
        jnp.where(position_rope < length, rope, added_rope),
    )


def attention_of(length, keys_ref, keys_rope_ref, q, q_rope, first=0):
    steps = q.shape[0]
    shape = (steps, HEADS, ROWS)
    seen = lax.broadcasted_iota(jnp.int32, shape, 2) <= length + first + lax.broadcasted_iota(jnp.int32, shape, 0)
    queries_rope = jnp.concatenate([q_rope[t].T for t in range(steps)], axis=0)
    scores = lax.dot_general(
        q.reshape(steps * HEADS, LATENT), keys_ref[...], (((1,), (1,)), ((), ())),
        preferred_element_type=jnp.float32,
    ) + jnp.dot(queries_rope, keys_rope_ref[...], preferred_element_type=jnp.float32)
    scores = jnp.where(seen.reshape(steps * HEADS, ROWS), scores * LOG2E_SCALE, -jnp.inf)
    raised = jnp.exp2(scores - jnp.max(scores, axis=1, keepdims=True))
    total = jnp.sum(raised, axis=1, keepdims=True)
    result = jnp.dot(raised.astype(jnp.bfloat16), keys_ref[...], preferred_element_type=jnp.float32)
    return (result * (1.0 / total)).astype(jnp.bfloat16).reshape(steps, HEADS, LATENT)


def exchange_kernel(
    dest_ref, length_ref, latent_ref, rope_ref, q_ref, q_rope_ref, new_ref, new_rope_ref,
    out_latent, out_rope, out_early, out_moved, out_moved_rope,
    held, staged, held_rope, staged_rope,
    q_early, q_rope_early, arrived, arrived_rope, early, moved, moved_rope,
    send_one, recv_one, send_two, recv_two,
    send_one_rope, recv_one_rope, send_two_rope, recv_two_rope,
    load_sem, store_sem,
):
    me = lax.axis_index("dp")
    place = rope_place(me)
    barrier = pltpu.get_barrier_semaphore()

    @pl.loop(1, RANKS)
    def _(k):
        pl.semaphore_signal(barrier, inc=1, device_id={"dp": shifted(me, k)}, device_id_type=MESH)

    pl.semaphore_wait(barrier, RANKS - 1)

    def send_rope(slot):
        @pl.loop(0, ROPE_UNITS)
        def _(i):
            q = (i + me) % ROPE_UNITS
            unit = slot * ROPE_UNITS + q
            peer, u = rope_rank(unit % RANKS), unit // RANKS
            source = rope_unit(rope_ref, slot, q)

            for w in range(2):
                if slot * ROPE_UNITS // RANKS <= w <= (slot * ROPE_UNITS + ROPE_UNITS - 1) // RANKS:
                    target = held_rope[w].at[me]

                    @pl.when((u == w) & (peer == me))
                    def _():
                        pltpu.make_async_copy(source, target, recv_one_rope.at[w]).start()

                    @pl.when((u == w) & (peer != me))
                    def _():
                        pltpu.make_async_remote_copy(
                            source, target, send_one_rope.at[slot], recv_one_rope.at[w],
                            device_id={"dp": peer}, device_id_type=MESH,
                        ).start()

    for slot in range(SLOTS):
        pltpu.make_async_copy(
            latent_piece(latent_ref, slot, me), held[slot].at[me], recv_one.at[slot]
        ).start()

        @pl.loop(1, RANKS)
        def _(k):
            peer = shifted(me, k)
            pltpu.make_async_remote_copy(
                latent_piece(latent_ref, slot, peer), held[slot].at[me],
                send_one.at[slot], recv_one.at[slot],
                device_id={"dp": peer}, device_id_type=MESH,
            ).start()

        send_rope(slot)

    load_q = pltpu.make_async_copy(q_ref.at[:, pl.ds(0, EARLY)], q_early, load_sem.at[0])
    load_q_rope = pltpu.make_async_copy(q_rope_ref.at[:, pl.ds(0, EARLY)], q_rope_early, load_sem.at[1])
    load_q.start()
    load_q_rope.start()

    def forward_rope(u):
        pltpu.make_async_copy(held_rope[u], held_rope[u], recv_one_rope.at[u]).wait()
        unit = place + RANKS * u
        slot, q = unit // ROPE_UNITS, unit % ROPE_UNITS

        @pl.loop(0, RANKS)
        def _(k):
            peer = shifted(me, k)
            origin = dest_ref[peer * SLOTS + slot]
            staged_rope[u, peer] = held_rope[u][origin]
            source, target = staged_rope.at[u, peer], rope_unit(out_rope, slot, q)

            @pl.when(k == 0)
            def _():
                pltpu.make_async_copy(source, target, recv_two_rope.at[slot]).start()

            @pl.when(k != 0)
            def _():
                pltpu.make_async_remote_copy(
                    source, target, send_two_rope.at[u], recv_two_rope.at[slot],
                    device_id={"dp": peer}, device_id_type=MESH,
                ).start()

    for slot in range(SLOTS):
        pltpu.make_async_copy(held[slot], held[slot], recv_one.at[slot]).wait()

        @pl.loop(0, RANKS)
        def _(k):
            peer = shifted(me, k)
            origin = dest_ref[peer * SLOTS + slot]
            staged[slot, peer] = held[slot][origin]
            source, target = staged.at[slot, peer], latent_piece(out_latent, slot, me)

            @pl.when(k == 0)
            def _():
                pltpu.make_async_copy(source, target, recv_two.at[slot]).start()

            @pl.when(k != 0)
            def _():
                pltpu.make_async_remote_copy(
                    source, target, send_two.at[slot], recv_two.at[slot],
                    device_id={"dp": peer}, device_id_type=MESH,
                ).start()

        for u in range(2):
            first, last = slot * ROPE_UNITS - RANKS * u, slot * ROPE_UNITS + ROPE_UNITS - RANKS * u
            first, last = max(first, 0), min(last, RANKS if u == 0 else 16)
            if first < last:
                pl.when((place >= first) & (place < last))(lambda u=u: forward_rope(u))

    def arrive(slot):
        pltpu.make_async_copy(out_latent.at[slot], out_latent.at[slot], recv_two.at[slot]).wait()
        pltpu.make_async_copy(out_rope.at[slot], out_rope.at[slot], recv_two_rope.at[slot]).wait()

    def stores(slot):
        return [
            pltpu.make_async_copy(early.at[slot], out_early.at[slot], store_sem.at[0, slot]),
            pltpu.make_async_copy(moved.at[slot], out_moved.at[slot], store_sem.at[1, slot]),
            pltpu.make_async_copy(moved_rope.at[slot], out_moved_rope.at[slot], store_sem.at[2, slot]),
        ]

    load_q.wait()
    load_q_rope.wait()
    for slot in range(EARLY):
        arrive(slot)
        load = pltpu.make_async_copy(out_latent.at[slot], arrived, load_sem.at[2])
        load_rope = pltpu.make_async_copy(out_rope.at[slot], arrived_rope, load_sem.at[3])
        load.start()
        load_rope.start()
        load.wait()
        load_rope.wait()
        length = length_ref[dest_ref[me * SLOTS + slot] * SLOTS + slot]
        moved[slot], moved_rope[slot] = merged(
            length, arrived[...], arrived_rope[...], new_ref[:, slot, :], new_rope_ref[:, slot, :]
        )
        early[slot] = attention_of(
            length, moved.at[slot], moved_rope.at[slot], q_early[:, slot], q_rope_early[:, slot]
        )
        for copy in stores(slot):
            copy.start()

    others = pl.ds(0, RANKS - 1)
    for slot in range(SLOTS):
        pltpu.make_async_copy(held[slot].at[others], held[slot].at[others], send_one.at[slot]).wait()
        own = place // ROPE_UNITS == slot
        own |= (place < 16) & ((place + RANKS) // ROPE_UNITS == slot)

        @pl.when(own)
        def _():
            part = held_rope[0].at[pl.ds(0, ROPE_UNITS - 1)]
            pltpu.make_async_copy(part, part, send_one_rope.at[slot]).wait()

        @pl.when(jnp.logical_not(own))
        def _():
            part = held_rope[0].at[pl.ds(0, ROPE_UNITS)]
            pltpu.make_async_copy(part, part, send_one_rope.at[slot]).wait()

    for slot in range(EARLY):
        for copy in stores(slot):
            copy.wait()
    for slot in range(SLOTS):
        pltpu.make_async_copy(staged.at[slot, others], staged.at[slot, others], send_two.at[slot]).wait()

    rest = staged_rope.at[0, others]
    pltpu.make_async_copy(rest, rest, send_two_rope.at[0]).wait()

    @pl.when(place < 16)
    def _():
        pltpu.make_async_copy(rest, rest, send_two_rope.at[1]).wait()

    for slot in range(EARLY, SLOTS):
        arrive(slot)


HBM = pl.BlockSpec(memory_space=pltpu.HBM)
ANY = pl.BlockSpec(memory_space=pl.ANY)
SMEM = pl.BlockSpec(memory_space=pltpu.SMEM)
VMEM = pl.BlockSpec(memory_space=pltpu.VMEM)


def like(*shape):
    return jax.ShapeDtypeStruct(shape, jnp.bfloat16)


def buffer(*shape):
    return pltpu.VMEM(shape, jnp.bfloat16)


def exchange(req_dest, req_length, latent_cache, rope_cache, q_latent, q_rope, new_latent, new_rope):
    dma = pltpu.SemaphoreType.DMA
    return pl.pallas_call(
        exchange_kernel,
        out_shape=(
            like(SLOTS, ROWS, LATENT), like(SLOTS, ROPE, ROWS),
            like(EARLY, STEPS, HEADS, LATENT), like(EARLY, ROWS, LATENT), like(EARLY, ROPE, ROWS),
        ),
        in_specs=[SMEM, SMEM, HBM, HBM, HBM, HBM, VMEM, VMEM],
        out_specs=(ANY,) * 5,
        scratch_shapes=[
            (buffer(RANKS, PIECE_ROWS, TILE),) * SLOTS,
            buffer(SLOTS, RANKS, PIECE_ROWS, TILE),
            (buffer(RANKS, 16, TILE),) * 2,
            buffer(2, RANKS, 16, TILE),
            buffer(STEPS, EARLY, HEADS, LATENT), buffer(STEPS, EARLY, ROPE, HEADS),
            buffer(ROWS, LATENT), buffer(ROPE, ROWS),
            buffer(EARLY, STEPS, HEADS, LATENT), buffer(EARLY, ROWS, LATENT), buffer(EARLY, ROPE, ROWS),
            dma((SLOTS,)), dma((SLOTS,)), dma((SLOTS,)), dma((SLOTS,)),
            dma((SLOTS,)), dma((2,)), dma((2,)), dma((SLOTS,)),
            dma((4,)), dma((3, EARLY)),
        ],
        compiler_params=pltpu.CompilerParams(
            collective_id=0, has_side_effects=True, vmem_limit_bytes=60 * 2**20
        ),
        cost_estimate=pl.CostEstimate(
            flops=2_600_000_000, bytes_accessed=16 * 2**20, transcendentals=1_200_000
        ),
        name="exchange",
    )(req_dest, req_length, latent_cache, rope_cache, q_latent, q_rope, new_latent, new_rope)


def finish_kernel(
    dest_ref, length_ref, latent_ref, rope_ref, early_ref, moved_ref, moved_rope_ref,
    q_ref, q_rope_ref, new_ref, new_rope_ref,
    out_ref, out_moved, out_moved_rope,
    latent, rope, q, q_rope, result, keys, keys_rope, early, moved, moved_rope, load_sem, store_sem,
):
    slot = EARLY
    loads = [
        pltpu.make_async_copy(latent_ref.at[slot], latent, load_sem.at[0]),
        pltpu.make_async_copy(rope_ref.at[slot], rope, load_sem.at[1]),
        pltpu.make_async_copy(q_ref.at[:, slot], q, load_sem.at[2]),
        pltpu.make_async_copy(q_rope_ref.at[:, slot], q_rope, load_sem.at[3]),
    ]
    for copy in loads:
        copy.start()
    fetches = [
        pltpu.make_async_copy(early_ref, early, load_sem.at[4]),
        pltpu.make_async_copy(moved_ref, moved, load_sem.at[5]),
        pltpu.make_async_copy(moved_rope_ref, moved_rope, load_sem.at[6]),
    ]
    copies = [
        pltpu.make_async_copy(early.at[k], out_ref.at[:, k], store_sem.at[k]) for k in range(EARLY)
    ] + [
        pltpu.make_async_copy(moved, out_moved.at[pl.ds(0, EARLY)], store_sem.at[EARLY]),
        pltpu.make_async_copy(moved_rope, out_moved_rope.at[pl.ds(0, EARLY)], store_sem.at[EARLY + 1]),
    ]
    for copy in fetches:
        copy.start()
    me = lax.axis_index("dp")
    length = length_ref[dest_ref[me * SLOTS + slot] * SLOTS + slot]
    loads[0].wait()
    loads[1].wait()
    keys[...], keys_rope[...] = merged(
        length, latent[...], rope[...], new_ref[:, slot, :], new_rope_ref[:, slot, :]
    )
    half = STEPS // 2
    own = [
        pltpu.make_async_copy(keys, out_moved.at[slot], store_sem.at[EARLY + 2]),
        pltpu.make_async_copy(keys_rope, out_moved_rope.at[slot], store_sem.at[EARLY + 3]),
    ] + [
        pltpu.make_async_copy(
            result.at[pl.ds(first, half)], out_ref.at[pl.ds(first, half), slot],
            store_sem.at[EARLY + 4 + first // half],
        )
        for first in (0, half)
    ]
    own[0].start()
    own[1].start()
    loads[2].wait()
    loads[3].wait()
    result[:half] = attention_of(length, keys, keys_rope, q[:half], q_rope[:half])
    own[2].start()
    for copy in fetches:
        copy.wait()
    for copy in copies:
        copy.start()
    result[half:] = attention_of(length, keys, keys_rope, q[half:], q_rope[half:], half)
    own[3].start()
    for copy in copies + own:
        copy.wait()


def finish(req_dest, req_length, exchanged, q_latent, q_rope, new_latent, new_rope):
    dma = pltpu.SemaphoreType.DMA
    return pl.pallas_call(
        finish_kernel,
        out_shape=(
            like(STEPS, SLOTS, HEADS, LATENT), like(SLOTS, ROWS, LATENT), like(SLOTS, ROPE, ROWS),
        ),
        in_specs=[SMEM, SMEM] + [ANY] * 5 + [HBM, HBM, VMEM, VMEM],
        out_specs=(HBM,) * 3,
        scratch_shapes=[
            buffer(ROWS, LATENT), buffer(ROPE, ROWS),
            buffer(STEPS, HEADS, LATENT), buffer(STEPS, ROPE, HEADS),
            buffer(STEPS, HEADS, LATENT), buffer(ROWS, LATENT), buffer(ROPE, ROWS),
            buffer(EARLY, STEPS, HEADS, LATENT), buffer(EARLY, ROWS, LATENT), buffer(EARLY, ROPE, ROWS),
            dma((7,)), dma((EARLY + 6,)),
        ],
        compiler_params=pltpu.CompilerParams(vmem_limit_bytes=60 * 2**20),
        cost_estimate=pl.CostEstimate(
            flops=900_000_000, bytes_accessed=12 * 2**20, transcendentals=400_000
        ),
        name="finish",
    )(req_dest, req_length, *exchanged, q_latent, q_rope, new_latent, new_rope)


def body(latent_cache, rope_cache, q_latent, q_rope, new_latent, new_rope, req_length, req_dest):
    queries = (q_latent, q_rope, new_latent, new_rope)
    exchanged = exchange(req_dest, req_length, latent_cache, rope_cache, *queries)
    return finish(req_dest, req_length, exchanged, *queries)


def solution(mesh):
    return jax.shard_map(
        body,
        mesh=mesh,
        in_specs=(
            P(("group", "dp"), None, None),
            P(("group", "dp"), None, None),
            P(None, ("group", "dp"), None, None),
            P(None, ("group", "dp"), None, None),
            P(None, ("group", "dp"), None),
            P(None, ("group", "dp"), None),
            P("group"),
            P("group"),
        ),
        out_specs=(
            P(None, ("group", "dp"), None, None),
            P(("group", "dp"), None, None),
            P(("group", "dp"), None, None),
        ),
        check_vma=False,
    )
```

```python
import math

import jax
import jax.numpy as jnp
from jax import lax
from jax.experimental import pallas as pl
from jax.experimental.pallas import tpu as pltpu
from jax.sharding import PartitionSpec as P

MESH = pl.DeviceIdType.MESH
RANKS = 32
RING = 8
SLOTS = 4
ROWS = 384
LATENT = 512
ROPE = 64
STEPS = 8
HEADS = 128
PIECE_ROWS = 48
TILE = 128
ROPE_UNITS = 12
EARLY = 3
LOG2E_SCALE = 192.0 ** (-0.5) * math.log2(math.e)


def shifted(rank, k):
    y, z = rank // RING, rank % RING
    return (y + k // RING) % 4 * RING + (z + 3 * k) % RING


def rope_place(rank):
    y, z = rank // RING, rank % RING
    return (y + z) % 2 * 16 + y * 4 + z // 2


def rope_rank(place):
    half, y, z = place // 16, place % 16 // 4, place % 4
    return y * RING + 2 * z + (y + half) % 2


def latent_piece(ref, slot, piece):
    row = pl.multiple_of(piece // 4 * PIECE_ROWS, PIECE_ROWS)
    column = pl.multiple_of(piece % 4 * TILE, TILE)
    return ref.at[slot, pl.ds(row, PIECE_ROWS), pl.ds(column, TILE)]


def rope_unit(ref, slot, unit):
    row = pl.multiple_of(unit % 4 * 16, 16)
    column = pl.multiple_of(unit // 4 * TILE, TILE)
    return ref.at[slot, pl.ds(row, 16), pl.ds(column, TILE)]


def merged(length, latent, rope, fresh, fresh_rope):
    row = lax.broadcasted_iota(jnp.int32, (ROWS, STEPS), 0)
    step = lax.broadcasted_iota(jnp.int32, (ROWS, STEPS), 1)
    placed = jnp.where(row - length == step, 1.0, 0.0).astype(jnp.bfloat16)
    added = jnp.dot(placed, fresh, preferred_element_type=jnp.float32).astype(jnp.bfloat16)
    position = lax.broadcasted_iota(jnp.int32, (ROWS, LATENT), 0)
    added_rope = lax.dot_general(
        fresh_rope, placed, (((0,), (1,)), ((), ())), preferred_element_type=jnp.float32
    ).astype(jnp.bfloat16)
    position_rope = lax.broadcasted_iota(jnp.int32, (ROPE, ROWS), 1)
    return (
        jnp.where(position < length, latent, added),
        jnp.where(position_rope < length, rope, added_rope),
    )


def turned(q_rope):
    return jnp.concatenate([q_rope[t].T for t in range(STEPS)], axis=0)


def attention_of(length, keys_ref, keys_rope_ref, q, q_rope, first=0):
    steps = q.shape[0]
    shape = (steps, HEADS, ROWS)
    seen = lax.broadcasted_iota(jnp.int32, shape, 2) <= length + first + lax.broadcasted_iota(jnp.int32, shape, 0)
    scores = lax.dot_general(
        q.reshape(steps * HEADS, LATENT), keys_ref[...], (((1,), (1,)), ((), ())),
        preferred_element_type=jnp.float32,
    ) + jnp.dot(q_rope, keys_rope_ref[...], preferred_element_type=jnp.float32)
    scores = jnp.where(seen.reshape(steps * HEADS, ROWS), scores * LOG2E_SCALE, -jnp.inf)
    raised = jnp.exp2(scores - jnp.max(scores, axis=1, keepdims=True))
    total = jnp.sum(raised, axis=1, keepdims=True)
    result = jnp.dot(raised.astype(jnp.bfloat16), keys_ref[...], preferred_element_type=jnp.float32)
    return (result * (1.0 / total)).astype(jnp.bfloat16).reshape(steps, HEADS, LATENT)


def exchange_kernel(
    dest_ref, length_ref, latent_ref, rope_ref, q_ref, q_rope_ref, new_ref, new_rope_ref,
    out_latent, out_rope, out_early, out_moved, out_moved_rope, out_q, out_q_rope,
    held, staged, held_rope, staged_rope,
    q_early, q_rope_all, q_turned, arrived, arrived_rope, early, moved, moved_rope,
    send_one, recv_one, send_two, recv_two,
    send_one_rope, recv_one_rope, send_two_rope, recv_two_rope,
    load_sem, store_sem,
):
    me = lax.axis_index("dp")
    place = rope_place(me)
    barrier = pltpu.get_barrier_semaphore()

    @pl.loop(1, RANKS)
    def _(k):
        pl.semaphore_signal(barrier, inc=1, device_id={"dp": shifted(me, k)}, device_id_type=MESH)

    pl.semaphore_wait(barrier, RANKS - 1)

    def send_rope(slot):
        @pl.loop(0, ROPE_UNITS)
        def _(i):
            q = (i + me) % ROPE_UNITS
            unit = slot * ROPE_UNITS + q
            peer, u = rope_rank(unit % RANKS), unit // RANKS
            source = rope_unit(rope_ref, slot, q)

            for w in range(2):
                if slot * ROPE_UNITS // RANKS <= w <= (slot * ROPE_UNITS + ROPE_UNITS - 1) // RANKS:
                    target = held_rope[w].at[me]

                    @pl.when((u == w) & (peer == me))
                    def _():
                        pltpu.make_async_copy(source, target, recv_one_rope.at[w]).start()

                    @pl.when((u == w) & (peer != me))
                    def _():
                        pltpu.make_async_remote_copy(
                            source, target, send_one_rope.at[slot], recv_one_rope.at[w],
                            device_id={"dp": peer}, device_id_type=MESH,
                        ).start()

    for slot in range(SLOTS):
        pltpu.make_async_copy(
            latent_piece(latent_ref, slot, me), held[slot].at[me], recv_one.at[slot]
        ).start()

        @pl.loop(1, RANKS)
        def _(k):
            peer = shifted(me, k)
            pltpu.make_async_remote_copy(
                latent_piece(latent_ref, slot, peer), held[slot].at[me],
                send_one.at[slot], recv_one.at[slot],
                device_id={"dp": peer}, device_id_type=MESH,
            ).start()

        send_rope(slot)

    load_q = pltpu.make_async_copy(q_ref.at[:, pl.ds(0, EARLY)], q_early, load_sem.at[0])
    load_q_rope = pltpu.make_async_copy(q_rope_ref, q_rope_all, load_sem.at[1])
    load_last = pltpu.make_async_copy(q_ref.at[:, EARLY], out_q, load_sem.at[4])
    load_last.start()
    load_q.start()
    load_q_rope.start()

    def forward_rope(u):
        pltpu.make_async_copy(held_rope[u], held_rope[u], recv_one_rope.at[u]).wait()
        unit = place + RANKS * u
        slot, q = unit // ROPE_UNITS, unit % ROPE_UNITS

        @pl.loop(0, RANKS)
        def _(k):
            peer = shifted(me, k)
            origin = dest_ref[peer * SLOTS + slot]
            staged_rope[u, peer] = held_rope[u][origin]
            source, target = staged_rope.at[u, peer], rope_unit(out_rope, slot, q)

            @pl.when(k == 0)
            def _():
                pltpu.make_async_copy(source, target, recv_two_rope.at[slot]).start()

            @pl.when(k != 0)
            def _():
                pltpu.make_async_remote_copy(
                    source, target, send_two_rope.at[u], recv_two_rope.at[slot],
                    device_id={"dp": peer}, device_id_type=MESH,
                ).start()

    for slot in range(SLOTS):
        pltpu.make_async_copy(held[slot], held[slot], recv_one.at[slot]).wait()

        @pl.loop(0, RANKS)
        def _(k):
            peer = shifted(me, k)
            origin = dest_ref[peer * SLOTS + slot]
            staged[slot, peer] = held[slot][origin]
            source, target = staged.at[slot, peer], latent_piece(out_latent, slot, me)

            @pl.when(k == 0)
            def _():
                pltpu.make_async_copy(source, target, recv_two.at[slot]).start()

            @pl.when(k != 0)
            def _():
                pltpu.make_async_remote_copy(
                    source, target, send_two.at[slot], recv_two.at[slot],
                    device_id={"dp": peer}, device_id_type=MESH,
                ).start()

        for u in range(2):
            first, last = slot * ROPE_UNITS - RANKS * u, slot * ROPE_UNITS + ROPE_UNITS - RANKS * u
            first, last = max(first, 0), min(last, RANKS if u == 0 else 16)
            if first < last:
                pl.when((place >= first) & (place < last))(lambda u=u: forward_rope(u))

    def arrive(slot):
        pltpu.make_async_copy(out_latent.at[slot], out_latent.at[slot], recv_two.at[slot]).wait()
        pltpu.make_async_copy(out_rope.at[slot], out_rope.at[slot], recv_two_rope.at[slot]).wait()

    def stores(slot):
        return [
            pltpu.make_async_copy(early.at[slot], out_early.at[slot], store_sem.at[0, slot]),
            pltpu.make_async_copy(moved.at[slot], out_moved.at[slot], store_sem.at[1, slot]),
            pltpu.make_async_copy(moved_rope.at[slot], out_moved_rope.at[slot], store_sem.at[2, slot]),
        ]

    load_q.wait()
    load_q_rope.wait()
    q_turned[...] = turned(q_rope_all[:, EARLY])
    store_turned = pltpu.make_async_copy(q_turned, out_q_rope, load_sem.at[5])
    store_turned.start()
    for slot in range(EARLY):
        arrive(slot)
        load = pltpu.make_async_copy(out_latent.at[slot], arrived, load_sem.at[2])
        load_rope = pltpu.make_async_copy(out_rope.at[slot], arrived_rope, load_sem.at[3])
        load.start()
        load_rope.start()
        load.wait()
        load_rope.wait()
        length = length_ref[dest_ref[me * SLOTS + slot] * SLOTS + slot]
        moved[slot], moved_rope[slot] = merged(
            length, arrived[...], arrived_rope[...], new_ref[:, slot, :], new_rope_ref[:, slot, :]
        )
        early[slot] = attention_of(
            length, moved.at[slot], moved_rope.at[slot], q_early[:, slot], turned(q_rope_all[:, slot])
        )
        for copy in stores(slot):
            copy.start()

    others = pl.ds(0, RANKS - 1)
    for slot in range(SLOTS):
        pltpu.make_async_copy(held[slot].at[others], held[slot].at[others], send_one.at[slot]).wait()
        own = place // ROPE_UNITS == slot
        own |= (place < 16) & ((place + RANKS) // ROPE_UNITS == slot)

        @pl.when(own)
        def _():
            part = held_rope[0].at[pl.ds(0, ROPE_UNITS - 1)]
            pltpu.make_async_copy(part, part, send_one_rope.at[slot]).wait()

        @pl.when(jnp.logical_not(own))
        def _():
            part = held_rope[0].at[pl.ds(0, ROPE_UNITS)]
            pltpu.make_async_copy(part, part, send_one_rope.at[slot]).wait()

    load_last.wait()
    store_turned.wait()
    for slot in range(EARLY):
        for copy in stores(slot):
            copy.wait()
    for slot in range(SLOTS):
        pltpu.make_async_copy(staged.at[slot, others], staged.at[slot, others], send_two.at[slot]).wait()

    rest = staged_rope.at[0, others]
    pltpu.make_async_copy(rest, rest, send_two_rope.at[0]).wait()

    @pl.when(place < 16)
    def _():
        pltpu.make_async_copy(rest, rest, send_two_rope.at[1]).wait()

    for slot in range(EARLY, SLOTS):
        arrive(slot)


HBM = pl.BlockSpec(memory_space=pltpu.HBM)
ANY = pl.BlockSpec(memory_space=pl.ANY)
SMEM = pl.BlockSpec(memory_space=pltpu.SMEM)
VMEM = pl.BlockSpec(memory_space=pltpu.VMEM)


def like(*shape):
    return jax.ShapeDtypeStruct(shape, jnp.bfloat16)


def buffer(*shape):
    return pltpu.VMEM(shape, jnp.bfloat16)


def exchange(req_dest, req_length, latent_cache, rope_cache, q_latent, q_rope, new_latent, new_rope):
    dma = pltpu.SemaphoreType.DMA
    return pl.pallas_call(
        exchange_kernel,
        out_shape=(
            buffer(SLOTS, ROWS, LATENT), buffer(SLOTS, ROPE, ROWS),
            buffer(EARLY, STEPS, HEADS, LATENT), buffer(EARLY, ROWS, LATENT), buffer(EARLY, ROPE, ROWS),
            buffer(STEPS, HEADS, LATENT), buffer(STEPS * HEADS, ROPE),
        ),
        in_specs=[SMEM, SMEM, HBM, HBM, HBM, HBM, VMEM, VMEM],
        out_specs=(ANY,) * 7,
        scratch_shapes=[
            (buffer(RANKS, PIECE_ROWS, TILE),) * SLOTS,
            buffer(SLOTS, RANKS, PIECE_ROWS, TILE),
            (buffer(RANKS, 16, TILE),) * 2,
            buffer(2, RANKS, 16, TILE),
            buffer(STEPS, EARLY, HEADS, LATENT), buffer(STEPS, SLOTS, ROPE, HEADS),
            buffer(STEPS * HEADS, ROPE),
            buffer(ROWS, LATENT), buffer(ROPE, ROWS),
            buffer(EARLY, STEPS, HEADS, LATENT), buffer(EARLY, ROWS, LATENT), buffer(EARLY, ROPE, ROWS),
            dma((SLOTS,)), dma((SLOTS,)), dma((SLOTS,)), dma((SLOTS,)),
            dma((SLOTS,)), dma((2,)), dma((2,)), dma((SLOTS,)),
            dma((6,)), dma((3, EARLY)),
        ],
        compiler_params=pltpu.CompilerParams(
            collective_id=0, has_side_effects=True, vmem_limit_bytes=32 * 2**20
        ),
        cost_estimate=pl.CostEstimate(
            flops=2_600_000_000, bytes_accessed=16 * 2**20, transcendentals=1_200_000
        ),
        name="exchange",
    )(req_dest, req_length, latent_cache, rope_cache, q_latent, q_rope, new_latent, new_rope)


def finish_kernel(
    dest_ref, length_ref, latent_ref, rope_ref, early_ref, moved_ref, moved_rope_ref,
    q, q_rope, new_ref, new_rope_ref,
    out_ref, out_moved, out_moved_rope,
    latent, rope, result, keys, keys_rope, load_sem, store_sem,
):
    slot = EARLY
    loads = [
        pltpu.make_async_copy(latent_ref.at[slot], latent, load_sem.at[0]),
        pltpu.make_async_copy(rope_ref.at[slot], rope, load_sem.at[1]),
    ]
    for copy in loads:
        copy.start()
    copies = [
        pltpu.make_async_copy(early_ref.at[k], out_ref.at[:, k], store_sem.at[k]) for k in range(EARLY)
    ] + [
        pltpu.make_async_copy(moved_ref, out_moved.at[pl.ds(0, EARLY)], store_sem.at[EARLY]),
        pltpu.make_async_copy(moved_rope_ref, out_moved_rope.at[pl.ds(0, EARLY)], store_sem.at[EARLY + 1]),
    ]
    for copy in copies:
        copy.start()
    me = lax.axis_index("dp")
    length = length_ref[dest_ref[me * SLOTS + slot] * SLOTS + slot]
    loads[0].wait()
    loads[1].wait()
    keys[...], keys_rope[...] = merged(
        length, latent[...], rope[...], new_ref[:, slot, :], new_rope_ref[:, slot, :]
    )
    half = STEPS // 2
    own = [
        pltpu.make_async_copy(keys, out_moved.at[slot], store_sem.at[EARLY + 2]),
        pltpu.make_async_copy(keys_rope, out_moved_rope.at[slot], store_sem.at[EARLY + 3]),
    ] + [
        pltpu.make_async_copy(
            result.at[pl.ds(first, half)], out_ref.at[pl.ds(first, half), slot],
            store_sem.at[EARLY + 4 + first // half],
        )
        for first in (0, half)
    ]
    own[0].start()
    own[1].start()
    result[:half] = attention_of(length, keys, keys_rope, q[:half], q_rope[: half * HEADS])
    own[2].start()
    result[half:] = attention_of(length, keys, keys_rope, q[half:], q_rope[half * HEADS :], half)
    own[3].start()
    for copy in copies + own:
        copy.wait()


def finish(req_dest, req_length, exchanged, new_latent, new_rope):
    dma = pltpu.SemaphoreType.DMA
    return pl.pallas_call(
        finish_kernel,
        out_shape=(
            like(STEPS, SLOTS, HEADS, LATENT), like(SLOTS, ROWS, LATENT), like(SLOTS, ROPE, ROWS),
        ),
        in_specs=[SMEM, SMEM] + [ANY] * 5 + [VMEM] * 4,
        out_specs=(HBM,) * 3,
        scratch_shapes=[
            buffer(ROWS, LATENT), buffer(ROPE, ROWS),
            buffer(STEPS, HEADS, LATENT), buffer(ROWS, LATENT), buffer(ROPE, ROWS),
            dma((2,)), dma((EARLY + 6,)),
        ],
        compiler_params=pltpu.CompilerParams(vmem_limit_bytes=20 * 2**20),
        cost_estimate=pl.CostEstimate(
            flops=900_000_000, bytes_accessed=12 * 2**20, transcendentals=400_000
        ),
        name="finish",
    )(req_dest, req_length, *exchanged, new_latent, new_rope)


def body(latent_cache, rope_cache, q_latent, q_rope, new_latent, new_rope, req_length, req_dest):
    in_hbm = lambda array: pltpu.with_memory_space_constraint(array, pltpu.HBM)
    latent_cache, rope_cache, req_dest, req_length = map(in_hbm, (latent_cache, rope_cache, req_dest, req_length))
    queries = tuple(map(in_hbm, (q_latent, q_rope, new_latent, new_rope)))
    exchanged = exchange(req_dest, req_length, latent_cache, rope_cache, *queries)
    return finish(req_dest, req_length, exchanged, *queries[2:])


def solution(mesh):
    return jax.shard_map(
        body,
        mesh=mesh,
        in_specs=(
            P(("group", "dp"), None, None),
            P(("group", "dp"), None, None),
            P(None, ("group", "dp"), None, None),
            P(None, ("group", "dp"), None, None),
            P(None, ("group", "dp"), None),
            P(None, ("group", "dp"), None),
            P("group"),
            P("group"),
        ),
        out_specs=(
            P(None, ("group", "dp"), None, None),
            P(("group", "dp"), None, None),
            P(("group", "dp"), None, None),
        ),
        check_vma=False,
    )
```

```python
import math

import jax
import jax.numpy as jnp
from jax import lax
from jax.experimental import pallas as pl
from jax.experimental.pallas import tpu as pltpu
from jax.sharding import PartitionSpec as P

MESH = pl.DeviceIdType.MESH
RANKS = 32
RING = 8
SLOTS = 4
ROWS = 384
LATENT = 512
ROPE = 64
STEPS = 8
HEADS = 128
PIECE_ROWS = 48
TILE = 128
ROPE_UNITS = 12
EARLY = 3
LOG2E_SCALE = 192.0 ** (-0.5) * math.log2(math.e)


def shifted(rank, k):
    y, z = rank // RING, rank % RING
    return (y + k // RING) % 4 * RING + (z + 3 * k) % RING


def rope_place(rank):
    y, z = rank // RING, rank % RING
    return (y + z) % 2 * 16 + y * 4 + z // 2


def rope_rank(place):
    half, y, z = place // 16, place % 16 // 4, place % 4
    return y * RING + 2 * z + (y + half) % 2


def latent_piece(ref, slot, piece):
    row = pl.multiple_of(piece // 4 * PIECE_ROWS, PIECE_ROWS)
    column = pl.multiple_of(piece % 4 * TILE, TILE)
    return ref.at[slot, pl.ds(row, PIECE_ROWS), pl.ds(column, TILE)]


def rope_unit(ref, slot, unit):
    row = pl.multiple_of(unit % 4 * 16, 16)
    column = pl.multiple_of(unit // 4 * TILE, TILE)
    return ref.at[slot, pl.ds(row, 16), pl.ds(column, TILE)]


def placed_new(length, fresh, fresh_rope):
    row = lax.broadcasted_iota(jnp.int32, (ROWS, STEPS), 0)
    step = lax.broadcasted_iota(jnp.int32, (ROWS, STEPS), 1)
    placed = jnp.where(row - length == step, 1.0, 0.0).astype(jnp.bfloat16)
    added = jnp.dot(placed, fresh, preferred_element_type=jnp.float32)
    added_rope = lax.dot_general(
        fresh_rope, placed, (((0,), (1,)), ((), ())), preferred_element_type=jnp.float32
    )
    return added.astype(jnp.bfloat16), added_rope.astype(jnp.bfloat16)


def merged(length, latent, rope, added, added_rope):
    position = lax.broadcasted_iota(jnp.int32, (ROWS, LATENT), 0)
    position_rope = lax.broadcasted_iota(jnp.int32, (ROPE, ROWS), 1)
    return (
        jnp.where(position < length, latent, added),
        jnp.where(position_rope < length, rope, added_rope),
    )


def turned(q_rope):
    return jnp.concatenate([q_rope[t].T for t in range(STEPS)], axis=0)


def attention_of(length, keys_ref, keys_rope_ref, q, q_rope, first=0):
    steps = q.shape[0]
    shape = (steps * HEADS, ROWS)
    step = first + lax.broadcasted_iota(jnp.int32, shape, 0) // HEADS
    seen = lax.broadcasted_iota(jnp.int32, shape, 1) - step <= length
    scores = lax.dot_general(
        q.reshape(steps * HEADS, LATENT), keys_ref[...], (((1,), (1,)), ((), ())),
        preferred_element_type=jnp.float32,
    ) + jnp.dot(q_rope, keys_rope_ref[...], preferred_element_type=jnp.float32)
    scores = jnp.where(seen, scores * LOG2E_SCALE, -jnp.inf)
    raised = jnp.exp2(scores - jnp.max(scores, axis=1, keepdims=True))
    total = jnp.sum(raised, axis=1, keepdims=True)
    result = jnp.dot(raised.astype(jnp.bfloat16), keys_ref[...], preferred_element_type=jnp.float32)
    return (result * (1.0 / total)).astype(jnp.bfloat16).reshape(steps, HEADS, LATENT)


def exchange_kernel(
    dest_hbm, length_hbm, latent_ref, rope_ref, q_ref, q_rope_ref, new_hbm, new_rope_hbm,
    out_latent, out_rope, out_early, out_moved, out_moved_rope, out_q, out_q_rope,
    out_added, out_added_rope, out_length,
    held, staged, held_rope, staged_rope,
    q_early, q_rope_all, q_turned, arrived, arrived_rope, early, moved, moved_rope,
    send_one, recv_one, send_two, recv_two,
    send_one_rope, recv_one_rope, send_two_rope, recv_two_rope,
    load_sem, store_sem, dest_ref, length_ref, new_ref, new_rope_ref, added, added_rope, length_row, small_sem,
):
    me = lax.axis_index("dp")
    place = rope_place(me)
    barrier = pltpu.get_barrier_semaphore()

    @pl.loop(1, RANKS)
    def _(k):
        pl.semaphore_signal(barrier, inc=1, device_id={"dp": shifted(me, k)}, device_id_type=MESH)

    small = [
        pltpu.make_async_copy(source, target, small_sem.at[i])
        for i, (source, target) in enumerate(
            ((dest_hbm, dest_ref), (length_hbm, length_ref), (new_hbm, new_ref), (new_rope_hbm, new_rope_ref))
        )
    ]
    for copy in small:
        copy.start()
    pl.semaphore_wait(barrier, RANKS - 1)

    def send_rope(slot):
        @pl.loop(0, ROPE_UNITS)
        def _(i):
            q = (i + me) % ROPE_UNITS
            unit = slot * ROPE_UNITS + q
            peer, u = rope_rank(unit % RANKS), unit // RANKS
            source = rope_unit(rope_ref, slot, q)

            for w in range(2):
                if slot * ROPE_UNITS // RANKS <= w <= (slot * ROPE_UNITS + ROPE_UNITS - 1) // RANKS:
                    target = held_rope[w].at[me]

                    @pl.when((u == w) & (peer == me))
                    def _():
                        pltpu.make_async_copy(source, target, recv_one_rope.at[w]).start()

                    @pl.when((u == w) & (peer != me))
                    def _():
                        pltpu.make_async_remote_copy(
                            source, target, send_one_rope.at[slot], recv_one_rope.at[w],
                            device_id={"dp": peer}, device_id_type=MESH,
                        ).start()

    for slot in range(SLOTS):
        pltpu.make_async_copy(
            latent_piece(latent_ref, slot, me), held[slot].at[me], recv_one.at[slot]
        ).start()

        @pl.loop(1, RANKS)
        def _(k):
            peer = shifted(me, k)
            pltpu.make_async_remote_copy(
                latent_piece(latent_ref, slot, peer), held[slot].at[me],
                send_one.at[slot], recv_one.at[slot],
                device_id={"dp": peer}, device_id_type=MESH,
            ).start()

        send_rope(slot)

    load_q = pltpu.make_async_copy(q_ref.at[:, pl.ds(0, EARLY)], q_early, load_sem.at[0])
    load_q_rope = pltpu.make_async_copy(q_rope_ref, q_rope_all, load_sem.at[1])
    load_last = pltpu.make_async_copy(q_ref.at[:, EARLY], out_q, load_sem.at[4])
    load_last.start()
    load_q.start()
    load_q_rope.start()

    def forward_rope(u):
        pltpu.make_async_copy(held_rope[u], held_rope[u], recv_one_rope.at[u]).wait()
        unit = place + RANKS * u
        slot, q = unit // ROPE_UNITS, unit % ROPE_UNITS

        @pl.loop(0, RANKS)
        def _(k):
            peer = shifted(me, k)
            origin = dest_ref[peer * SLOTS + slot]
            staged_rope[u, peer] = held_rope[u][origin]
            source, target = staged_rope.at[u, peer], rope_unit(out_rope, slot, q)

            @pl.when(k == 0)
            def _():
                pltpu.make_async_copy(source, target, recv_two_rope.at[slot]).start()

            @pl.when(k != 0)
            def _():
                pltpu.make_async_remote_copy(
                    source, target, send_two_rope.at[u], recv_two_rope.at[slot],
                    device_id={"dp": peer}, device_id_type=MESH,
                ).start()

    for copy in small:
        copy.wait()
    for slot in range(SLOTS):
        pltpu.make_async_copy(held[slot], held[slot], recv_one.at[slot]).wait()

        @pl.loop(0, RANKS)
        def _(k):
            peer = shifted(me, k)
            origin = dest_ref[peer * SLOTS + slot]
            staged[slot, peer] = held[slot][origin]
            source, target = staged.at[slot, peer], latent_piece(out_latent, slot, me)

            @pl.when(k == 0)
            def _():
                pltpu.make_async_copy(source, target, recv_two.at[slot]).start()

            @pl.when(k != 0)
            def _():
                pltpu.make_async_remote_copy(
                    source, target, send_two.at[slot], recv_two.at[slot],
                    device_id={"dp": peer}, device_id_type=MESH,
                ).start()

        for u in range(2):
            first, last = slot * ROPE_UNITS - RANKS * u, slot * ROPE_UNITS + ROPE_UNITS - RANKS * u
            first, last = max(first, 0), min(last, RANKS if u == 0 else 16)
            if first < last:
                pl.when((place >= first) & (place < last))(lambda u=u: forward_rope(u))

    def arrive(slot):
        pltpu.make_async_copy(out_latent.at[slot], out_latent.at[slot], recv_two.at[slot]).wait()
        pltpu.make_async_copy(out_rope.at[slot], out_rope.at[slot], recv_two_rope.at[slot]).wait()

    def stores(slot):
        return [
            pltpu.make_async_copy(early.at[slot], out_early.at[slot], store_sem.at[0, slot]),
            pltpu.make_async_copy(moved.at[slot], out_moved.at[slot], store_sem.at[1, slot]),
            pltpu.make_async_copy(moved_rope.at[slot], out_moved_rope.at[slot], store_sem.at[2, slot]),
        ]

    load_q.wait()
    load_q_rope.wait()
    q_turned[...] = turned(q_rope_all[:, EARLY])
    store_turned = pltpu.make_async_copy(q_turned, out_q_rope, load_sem.at[5])
    store_turned.start()
    last_length = length_ref[dest_ref[me * SLOTS + EARLY] * SLOTS + EARLY]
    added[...], added_rope[...] = placed_new(last_length, new_ref[:, EARLY, :], new_rope_ref[:, EARLY, :])
    length_row[...] = jnp.full((8, TILE), last_length, jnp.int32)
    last = [
        pltpu.make_async_copy(added, out_added, load_sem.at[6]),
        pltpu.make_async_copy(added_rope, out_added_rope, load_sem.at[7]),
        pltpu.make_async_copy(length_row, out_length, load_sem.at[8]),
    ]
    for copy in last:
        copy.start()
    for slot in range(EARLY):
        arrive(slot)
        load = pltpu.make_async_copy(out_latent.at[slot], arrived, load_sem.at[2])
        load_rope = pltpu.make_async_copy(out_rope.at[slot], arrived_rope, load_sem.at[3])
        load.start()
        load_rope.start()
        load.wait()
        load_rope.wait()
        length = length_ref[dest_ref[me * SLOTS + slot] * SLOTS + slot]
        moved[slot], moved_rope[slot] = merged(
            length, arrived[...], arrived_rope[...],
            *placed_new(length, new_ref[:, slot, :], new_rope_ref[:, slot, :]),
        )
        early[slot] = attention_of(
            length, moved.at[slot], moved_rope.at[slot], q_early[:, slot], turned(q_rope_all[:, slot])
        )
        for copy in stores(slot):
            copy.start()

    others = pl.ds(0, RANKS - 1)
    for slot in range(SLOTS):
        pltpu.make_async_copy(held[slot].at[others], held[slot].at[others], send_one.at[slot]).wait()
        own = place // ROPE_UNITS == slot
        own |= (place < 16) & ((place + RANKS) // ROPE_UNITS == slot)

        @pl.when(own)
        def _():
            part = held_rope[0].at[pl.ds(0, ROPE_UNITS - 1)]
            pltpu.make_async_copy(part, part, send_one_rope.at[slot]).wait()

        @pl.when(jnp.logical_not(own))
        def _():
            part = held_rope[0].at[pl.ds(0, ROPE_UNITS)]
            pltpu.make_async_copy(part, part, send_one_rope.at[slot]).wait()

    load_last.wait()
    store_turned.wait()
    for copy in last:
        copy.wait()
    for slot in range(EARLY):
        for copy in stores(slot):
            copy.wait()
    for slot in range(SLOTS):
        pltpu.make_async_copy(staged.at[slot, others], staged.at[slot, others], send_two.at[slot]).wait()

    rest = staged_rope.at[0, others]
    pltpu.make_async_copy(rest, rest, send_two_rope.at[0]).wait()

    @pl.when(place < 16)
    def _():
        pltpu.make_async_copy(rest, rest, send_two_rope.at[1]).wait()

    for slot in range(EARLY, SLOTS):
        arrive(slot)


HBM = pl.BlockSpec(memory_space=pltpu.HBM)
ANY = pl.BlockSpec(memory_space=pl.ANY)
VMEM = pl.BlockSpec(memory_space=pltpu.VMEM)


def like(*shape):
    return jax.ShapeDtypeStruct(shape, jnp.bfloat16)


def buffer(*shape):
    return pltpu.VMEM(shape, jnp.bfloat16)


def exchange(req_dest, req_length, latent_cache, rope_cache, q_latent, q_rope, new_latent, new_rope):
    dma = pltpu.SemaphoreType.DMA
    return pl.pallas_call(
        exchange_kernel,
        out_shape=(
            buffer(SLOTS, ROWS, LATENT), buffer(SLOTS, ROPE, ROWS),
            buffer(EARLY, STEPS, HEADS, LATENT), buffer(EARLY, ROWS, LATENT), buffer(EARLY, ROPE, ROWS),
            buffer(STEPS, HEADS, LATENT), buffer(STEPS * HEADS, ROPE),
            buffer(ROWS, LATENT), buffer(ROPE, ROWS), pltpu.VMEM((8, TILE), jnp.int32),
        ),
        in_specs=[HBM] * 8,
        out_specs=(ANY,) * 10,
        scratch_shapes=[
            (buffer(RANKS, PIECE_ROWS, TILE),) * SLOTS,
            buffer(SLOTS, RANKS, PIECE_ROWS, TILE),
            (buffer(RANKS, 16, TILE),) * 2,
            buffer(2, RANKS, 16, TILE),
            buffer(STEPS, EARLY, HEADS, LATENT), buffer(STEPS, SLOTS, ROPE, HEADS),
            buffer(STEPS * HEADS, ROPE),
            buffer(ROWS, LATENT), buffer(ROPE, ROWS),
            buffer(EARLY, STEPS, HEADS, LATENT), buffer(EARLY, ROWS, LATENT), buffer(EARLY, ROPE, ROWS),
            dma((SLOTS,)), dma((SLOTS,)), dma((SLOTS,)), dma((SLOTS,)),
            dma((SLOTS,)), dma((2,)), dma((2,)), dma((SLOTS,)),
            dma((9,)), dma((3, EARLY)),
            pltpu.SMEM(req_dest.shape, jnp.int32), pltpu.SMEM(req_length.shape, jnp.int32),
            buffer(*new_latent.shape), buffer(*new_rope.shape),
            buffer(ROWS, LATENT), buffer(ROPE, ROWS), pltpu.VMEM((8, TILE), jnp.int32), dma((4,)),
        ],
        compiler_params=pltpu.CompilerParams(
            collective_id=0, has_side_effects=True, vmem_limit_bytes=32 * 2**20
        ),
        cost_estimate=pl.CostEstimate(
            flops=2_600_000_000, bytes_accessed=16 * 2**20, transcendentals=1_200_000
        ),
        name="exchange",
    )(req_dest, req_length, latent_cache, rope_cache, q_latent, q_rope, new_latent, new_rope)


def finish_kernel(
    latent_ref, rope_ref, early_ref, moved_ref, moved_rope_ref, q, q_rope, added, added_rope, length_ref,
    out_ref, out_moved, out_moved_rope,
    result, keys, keys_rope, store_sem,
):
    slot = EARLY
    copies = [
        pltpu.make_async_copy(early_ref.at[k], out_ref.at[:, k], store_sem.at[k]) for k in range(EARLY)
    ] + [
        pltpu.make_async_copy(moved_ref, out_moved.at[pl.ds(0, EARLY)], store_sem.at[EARLY]),
        pltpu.make_async_copy(moved_rope_ref, out_moved_rope.at[pl.ds(0, EARLY)], store_sem.at[EARLY + 1]),
    ]
    for copy in copies:
        copy.start()
    length = length_ref[:1, :1]
    keys[...], keys_rope[...] = merged(length, latent_ref[slot], rope_ref[slot], added[...], added_rope[...])
    half = STEPS // 2
    own = [
        pltpu.make_async_copy(keys, out_moved.at[slot], store_sem.at[EARLY + 2]),
        pltpu.make_async_copy(keys_rope, out_moved_rope.at[slot], store_sem.at[EARLY + 3]),
    ] + [
        pltpu.make_async_copy(
            result.at[pl.ds(first, half)], out_ref.at[pl.ds(first, half), slot],
            store_sem.at[EARLY + 4 + first // half],
        )
        for first in (0, half)
    ]
    own[0].start()
    own[1].start()
    result[:half] = attention_of(length, keys, keys_rope, q[:half], q_rope[: half * HEADS])
    own[2].start()
    result[half:] = attention_of(length, keys, keys_rope, q[half:], q_rope[half * HEADS :], half)
    own[3].start()
    for copy in copies + own:
        copy.wait()


def finish(exchanged):
    dma = pltpu.SemaphoreType.DMA
    return pl.pallas_call(
        finish_kernel,
        out_shape=(
            like(STEPS, SLOTS, HEADS, LATENT), like(SLOTS, ROWS, LATENT), like(SLOTS, ROPE, ROWS),
        ),
        in_specs=[VMEM] * 2 + [ANY] * 3 + [VMEM] * 5,
        out_specs=(HBM,) * 3,
        scratch_shapes=[
            buffer(STEPS, HEADS, LATENT), buffer(ROWS, LATENT), buffer(ROPE, ROWS), dma((EARLY + 6,)),
        ],
        compiler_params=pltpu.CompilerParams(vmem_limit_bytes=20 * 2**20),
        cost_estimate=pl.CostEstimate(
            flops=900_000_000, bytes_accessed=12 * 2**20, transcendentals=400_000
        ),
        name="finish",
    )(*exchanged)


def body(latent_cache, rope_cache, q_latent, q_rope, new_latent, new_rope, req_length, req_dest):
    in_hbm = lambda array: pltpu.with_memory_space_constraint(array, pltpu.HBM)
    latent_cache, rope_cache, req_dest, req_length = map(in_hbm, (latent_cache, rope_cache, req_dest, req_length))
    queries = tuple(map(in_hbm, (q_latent, q_rope, new_latent, new_rope)))
    exchanged = exchange(req_dest, req_length, latent_cache, rope_cache, *queries)
    return finish(exchanged)


def solution(mesh):
    return jax.shard_map(
        body,
        mesh=mesh,
        in_specs=(
            P(("group", "dp"), None, None),
            P(("group", "dp"), None, None),
            P(None, ("group", "dp"), None, None),
            P(None, ("group", "dp"), None, None),
            P(None, ("group", "dp"), None),
            P(None, ("group", "dp"), None),
            P("group"),
            P("group"),
        ),
        out_specs=(
            P(None, ("group", "dp"), None, None),
            P(("group", "dp"), None, None),
            P(("group", "dp"), None, None),
        ),
        check_vma=False,
    )
```

```python
import math

import jax
import jax.numpy as jnp
from jax import lax
from jax.experimental import pallas as pl
from jax.experimental.pallas import tpu as pltpu
from jax.sharding import PartitionSpec as P

MESH = pl.DeviceIdType.MESH
RANKS = 32
RING = 8
SLOTS = 4
ROWS = 384
LATENT = 512
ROPE = 64
STEPS = 8
HEADS = 128
PIECE_ROWS = 48
TILE = 128
ROPE_UNITS = 12
EARLY = 3
LOG2E_SCALE = 192.0 ** (-0.5) * math.log2(math.e)


def shifted(rank, k):
    y, z = rank // RING, rank % RING
    return (y + k // RING) % 4 * RING + (z + 3 * k) % RING


def rope_place(rank):
    y, z = rank // RING, rank % RING
    return (y + z) % 2 * 16 + y * 4 + z // 2


def rope_rank(place):
    half, y, z = place // 16, place % 16 // 4, place % 4
    return y * RING + 2 * z + (y + half) % 2


def latent_piece(ref, slot, piece):
    row = pl.multiple_of(piece // 4 * PIECE_ROWS, PIECE_ROWS)
    column = pl.multiple_of(piece % 4 * TILE, TILE)
    return ref.at[slot, pl.ds(row, PIECE_ROWS), pl.ds(column, TILE)]


def rope_unit(ref, slot, unit):
    row = pl.multiple_of(unit % 4 * 16, 16)
    column = pl.multiple_of(unit // 4 * TILE, TILE)
    return ref.at[slot, pl.ds(row, 16), pl.ds(column, TILE)]


def placed_new(length, fresh, fresh_rope):
    row = lax.broadcasted_iota(jnp.int32, (ROWS, STEPS), 0)
    step = lax.broadcasted_iota(jnp.int32, (ROWS, STEPS), 1)
    placed = jnp.where(row - length == step, 1.0, 0.0).astype(jnp.bfloat16)
    added = jnp.dot(placed, fresh, preferred_element_type=jnp.float32)
    added_rope = lax.dot_general(
        fresh_rope, placed, (((0,), (1,)), ((), ())), preferred_element_type=jnp.float32
    )
    return added.astype(jnp.bfloat16), added_rope.astype(jnp.bfloat16)


def merged(length, latent, rope, added, added_rope):
    position = lax.broadcasted_iota(jnp.int32, (ROWS, LATENT), 0)
    position_rope = lax.broadcasted_iota(jnp.int32, (ROPE, ROWS), 1)
    return (
        jnp.where(position < length, latent, added),
        jnp.where(position_rope < length, rope, added_rope),
    )


def turned(q_rope):
    return jnp.concatenate([q_rope[t].T for t in range(STEPS)], axis=0)


def scores_of(length, keys_ref, keys_rope_ref, q, q_rope, first=0):
    steps = q.shape[0]
    shape = (steps * HEADS, ROWS)
    step = first + lax.broadcasted_iota(jnp.int32, shape, 0) // HEADS
    seen = lax.broadcasted_iota(jnp.int32, shape, 1) - step <= length
    scores = lax.dot_general(
        q.reshape(steps * HEADS, LATENT), keys_ref[...], (((1,), (1,)), ((), ())),
        preferred_element_type=jnp.float32,
    ) + jnp.dot(q_rope, keys_rope_ref[...], preferred_element_type=jnp.float32)
    return jnp.where(seen, scores * LOG2E_SCALE, -jnp.inf)


def weighted(scores, keys_ref):
    raised = jnp.exp2(scores - jnp.max(scores, axis=1, keepdims=True))
    total = jnp.sum(raised, axis=1, keepdims=True)
    result = jnp.dot(raised.astype(jnp.bfloat16), keys_ref[...], preferred_element_type=jnp.float32)
    return (result * (1.0 / total)).astype(jnp.bfloat16).reshape(-1, HEADS, LATENT)


def attention_of(length, keys_ref, keys_rope_ref, q, q_rope):
    return weighted(scores_of(length, keys_ref, keys_rope_ref, q, q_rope), keys_ref)


def exchange_kernel(
    dest_hbm, length_hbm, latent_ref, rope_ref, q_ref, q_rope_ref, new_hbm, new_rope_hbm,
    out_latent, out_rope, out_early, out_moved, out_moved_rope, out_q, out_q_rope,
    out_added, out_added_rope, out_length,
    held, staged, held_rope, staged_rope,
    q_early, q_rope_all, q_turned, arrived, arrived_rope, early, moved, moved_rope,
    send_one, recv_one, send_two, recv_two,
    send_one_rope, recv_one_rope, send_two_rope, recv_two_rope,
    load_sem, store_sem, dest_ref, length_ref, new_ref, new_rope_ref, added, added_rope, length_row, small_sem,
):
    me = lax.axis_index("dp")
    place = rope_place(me)
    barrier = pltpu.get_barrier_semaphore()

    @pl.loop(1, RANKS)
    def _(k):
        pl.semaphore_signal(barrier, inc=1, device_id={"dp": shifted(me, k)}, device_id_type=MESH)

    small = [
        pltpu.make_async_copy(source, target, small_sem.at[i])
        for i, (source, target) in enumerate(
            ((dest_hbm, dest_ref), (length_hbm, length_ref), (new_hbm, new_ref), (new_rope_hbm, new_rope_ref))
        )
    ]
    for copy in small:
        copy.start()
    pl.semaphore_wait(barrier, RANKS - 1)

    def send_rope(slot):
        @pl.loop(0, ROPE_UNITS)
        def _(i):
            q = (i + me) % ROPE_UNITS
            unit = slot * ROPE_UNITS + q
            peer, u = rope_rank(unit % RANKS), unit // RANKS
            source = rope_unit(rope_ref, slot, q)

            for w in range(2):
                if slot * ROPE_UNITS // RANKS <= w <= (slot * ROPE_UNITS + ROPE_UNITS - 1) // RANKS:
                    target = held_rope[w].at[me]

                    @pl.when((u == w) & (peer == me))
                    def _():
                        pltpu.make_async_copy(source, target, recv_one_rope.at[w]).start()

                    @pl.when((u == w) & (peer != me))
                    def _():
                        pltpu.make_async_remote_copy(
                            source, target, send_one_rope.at[slot], recv_one_rope.at[w],
                            device_id={"dp": peer}, device_id_type=MESH,
                        ).start()

    for slot in range(SLOTS):
        send_rope(slot)
        pltpu.make_async_copy(
            latent_piece(latent_ref, slot, me), held[slot].at[me], recv_one.at[slot]
        ).start()

        @pl.loop(1, RANKS)
        def _(k):
            peer = shifted(me, k)
            pltpu.make_async_remote_copy(
                latent_piece(latent_ref, slot, peer), held[slot].at[me],
                send_one.at[slot], recv_one.at[slot],
                device_id={"dp": peer}, device_id_type=MESH,
            ).start()

    load_q = pltpu.make_async_copy(q_ref.at[:, pl.ds(0, EARLY)], q_early, load_sem.at[0])
    load_q_rope = pltpu.make_async_copy(q_rope_ref, q_rope_all, load_sem.at[1])
    load_last = pltpu.make_async_copy(q_ref.at[:, EARLY], out_q, load_sem.at[4])
    load_last.start()
    load_q.start()
    load_q_rope.start()

    def forward_rope(u):
        pltpu.make_async_copy(held_rope[u], held_rope[u], recv_one_rope.at[u]).wait()
        unit = place + RANKS * u
        slot, q = unit // ROPE_UNITS, unit % ROPE_UNITS

        @pl.loop(0, RANKS)
        def _(k):
            peer = shifted(me, k)
            origin = dest_ref[peer * SLOTS + slot]
            staged_rope[u, peer] = held_rope[u][origin]
            source, target = staged_rope.at[u, peer], rope_unit(out_rope, slot, q)

            @pl.when(k == 0)
            def _():
                pltpu.make_async_copy(source, target, recv_two_rope.at[slot]).start()

            @pl.when(k != 0)
            def _():
                pltpu.make_async_remote_copy(
                    source, target, send_two_rope.at[u], recv_two_rope.at[slot],
                    device_id={"dp": peer}, device_id_type=MESH,
                ).start()

    for copy in small:
        copy.wait()
    for slot in range(SLOTS):
        for u in range(2):
            first, last = slot * ROPE_UNITS - RANKS * u, slot * ROPE_UNITS + ROPE_UNITS - RANKS * u
            first, last = max(first, 0), min(last, RANKS if u == 0 else 16)
            if first < last:
                pl.when((place >= first) & (place < last))(lambda u=u: forward_rope(u))

        pltpu.make_async_copy(held[slot], held[slot], recv_one.at[slot]).wait()

        @pl.loop(0, RANKS)
        def _(k):
            peer = shifted(me, k)
            origin = dest_ref[peer * SLOTS + slot]
            staged[slot, peer] = held[slot][origin]
            source, target = staged.at[slot, peer], latent_piece(out_latent, slot, me)

            @pl.when(k == 0)
            def _():
                pltpu.make_async_copy(source, target, recv_two.at[slot]).start()

            @pl.when(k != 0)
            def _():
                pltpu.make_async_remote_copy(
                    source, target, send_two.at[slot], recv_two.at[slot],
                    device_id={"dp": peer}, device_id_type=MESH,
                ).start()

    def arrive(slot):
        pltpu.make_async_copy(out_latent.at[slot], out_latent.at[slot], recv_two.at[slot]).wait()
        pltpu.make_async_copy(out_rope.at[slot], out_rope.at[slot], recv_two_rope.at[slot]).wait()

    def stores(slot):
        return [
            pltpu.make_async_copy(early.at[slot], out_early.at[slot], store_sem.at[0, slot]),
            pltpu.make_async_copy(moved.at[slot], out_moved.at[slot], store_sem.at[1, slot]),
            pltpu.make_async_copy(moved_rope.at[slot], out_moved_rope.at[slot], store_sem.at[2, slot]),
        ]

    load_q.wait()
    load_q_rope.wait()
    q_turned[...] = turned(q_rope_all[:, EARLY])
    store_turned = pltpu.make_async_copy(q_turned, out_q_rope, load_sem.at[5])
    store_turned.start()
    last_length = length_ref[dest_ref[me * SLOTS + EARLY] * SLOTS + EARLY]
    added[...], added_rope[...] = placed_new(last_length, new_ref[:, EARLY, :], new_rope_ref[:, EARLY, :])
    length_row[...] = jnp.full((8, TILE), last_length, jnp.int32)
    last = [
        pltpu.make_async_copy(added, out_added, load_sem.at[6]),
        pltpu.make_async_copy(added_rope, out_added_rope, load_sem.at[7]),
        pltpu.make_async_copy(length_row, out_length, load_sem.at[8]),
    ]
    for copy in last:
        copy.start()
    for slot in range(EARLY):
        arrive(slot)
        load = pltpu.make_async_copy(out_latent.at[slot], arrived, load_sem.at[2])
        load_rope = pltpu.make_async_copy(out_rope.at[slot], arrived_rope, load_sem.at[3])
        load.start()
        load_rope.start()
        load.wait()
        load_rope.wait()
        length = length_ref[dest_ref[me * SLOTS + slot] * SLOTS + slot]
        moved[slot], moved_rope[slot] = merged(
            length, arrived[...], arrived_rope[...],
            *placed_new(length, new_ref[:, slot, :], new_rope_ref[:, slot, :]),
        )
        early[slot] = attention_of(
            length, moved.at[slot], moved_rope.at[slot], q_early[:, slot], turned(q_rope_all[:, slot])
        )
        for copy in stores(slot):
            copy.start()

    others = pl.ds(0, RANKS - 1)
    for slot in range(SLOTS):
        pltpu.make_async_copy(held[slot].at[others], held[slot].at[others], send_one.at[slot]).wait()
        own = place // ROPE_UNITS == slot
        own |= (place < 16) & ((place + RANKS) // ROPE_UNITS == slot)

        @pl.when(own)
        def _():
            part = held_rope[0].at[pl.ds(0, ROPE_UNITS - 1)]
            pltpu.make_async_copy(part, part, send_one_rope.at[slot]).wait()

        @pl.when(jnp.logical_not(own))
        def _():
            part = held_rope[0].at[pl.ds(0, ROPE_UNITS)]
            pltpu.make_async_copy(part, part, send_one_rope.at[slot]).wait()

    load_last.wait()
    store_turned.wait()
    for copy in last:
        copy.wait()
    for slot in range(EARLY):
        for copy in stores(slot):
            copy.wait()
    for slot in range(SLOTS):
        pltpu.make_async_copy(staged.at[slot, others], staged.at[slot, others], send_two.at[slot]).wait()

    rest = staged_rope.at[0, others]
    pltpu.make_async_copy(rest, rest, send_two_rope.at[0]).wait()

    @pl.when(place < 16)
    def _():
        pltpu.make_async_copy(rest, rest, send_two_rope.at[1]).wait()

    for slot in range(EARLY, SLOTS):
        arrive(slot)


HBM = pl.BlockSpec(memory_space=pltpu.HBM)
ANY = pl.BlockSpec(memory_space=pl.ANY)
VMEM = pl.BlockSpec(memory_space=pltpu.VMEM)


def like(*shape):
    return jax.ShapeDtypeStruct(shape, jnp.bfloat16)


def buffer(*shape):
    return pltpu.VMEM(shape, jnp.bfloat16)


def exchange(req_dest, req_length, latent_cache, rope_cache, q_latent, q_rope, new_latent, new_rope):
    dma = pltpu.SemaphoreType.DMA
    return pl.pallas_call(
        exchange_kernel,
        out_shape=(
            buffer(SLOTS, ROWS, LATENT), buffer(SLOTS, ROPE, ROWS),
            buffer(EARLY, STEPS, HEADS, LATENT), buffer(EARLY, ROWS, LATENT), buffer(EARLY, ROPE, ROWS),
            buffer(STEPS, HEADS, LATENT), buffer(STEPS * HEADS, ROPE),
            buffer(ROWS, LATENT), buffer(ROPE, ROWS), pltpu.VMEM((8, TILE), jnp.int32),
        ),
        in_specs=[HBM] * 8,
        out_specs=(ANY,) * 10,
        scratch_shapes=[
            (buffer(RANKS, PIECE_ROWS, TILE),) * SLOTS,
            buffer(SLOTS, RANKS, PIECE_ROWS, TILE),
            (buffer(RANKS, 16, TILE),) * 2,
            buffer(2, RANKS, 16, TILE),
            buffer(STEPS, EARLY, HEADS, LATENT), buffer(STEPS, SLOTS, ROPE, HEADS),
            buffer(STEPS * HEADS, ROPE),
            buffer(ROWS, LATENT), buffer(ROPE, ROWS),
            buffer(EARLY, STEPS, HEADS, LATENT), buffer(EARLY, ROWS, LATENT), buffer(EARLY, ROPE, ROWS),
            dma((SLOTS,)), dma((SLOTS,)), dma((SLOTS,)), dma((SLOTS,)),
            dma((SLOTS,)), dma((2,)), dma((2,)), dma((SLOTS,)),
            dma((9,)), dma((3, EARLY)),
            pltpu.SMEM(req_dest.shape, jnp.int32), pltpu.SMEM(req_length.shape, jnp.int32),
            buffer(*new_latent.shape), buffer(*new_rope.shape),
            buffer(ROWS, LATENT), buffer(ROPE, ROWS), pltpu.VMEM((8, TILE), jnp.int32), dma((4,)),
        ],
        compiler_params=pltpu.CompilerParams(
            collective_id=0, has_side_effects=True, vmem_limit_bytes=32 * 2**20
        ),
        cost_estimate=pl.CostEstimate(
            flops=2_600_000_000, bytes_accessed=16 * 2**20, transcendentals=1_200_000
        ),
        name="exchange",
    )(req_dest, req_length, latent_cache, rope_cache, q_latent, q_rope, new_latent, new_rope)


def finish_kernel(
    latent_ref, rope_ref, early_ref, moved_ref, moved_rope_ref, q, q_rope, added, added_rope, length_ref,
    out_ref, out_moved, out_moved_rope,
    result, keys, keys_rope, store_sem,
):
    slot = EARLY
    copies = [
        pltpu.make_async_copy(early_ref.at[k], out_ref.at[:, k], store_sem.at[k]) for k in range(EARLY)
    ] + [
        pltpu.make_async_copy(moved_ref, out_moved.at[pl.ds(0, EARLY)], store_sem.at[EARLY]),
        pltpu.make_async_copy(moved_rope_ref, out_moved_rope.at[pl.ds(0, EARLY)], store_sem.at[EARLY + 1]),
    ]
    for copy in copies:
        copy.start()
    length = length_ref[:1, :1]
    keys[...], keys_rope[...] = merged(length, latent_ref[slot], rope_ref[slot], added[...], added_rope[...])
    part = STEPS // 2
    own = [
        pltpu.make_async_copy(keys, out_moved.at[slot], store_sem.at[EARLY + 2]),
        pltpu.make_async_copy(keys_rope, out_moved_rope.at[slot], store_sem.at[EARLY + 3]),
    ]
    own[0].start()
    own[1].start()
    scores = [
        scores_of(length, keys, keys_rope, q[k : k + part], q_rope[k * HEADS : (k + part) * HEADS], k)
        for k in range(0, STEPS, part)
    ]
    for i, k in enumerate(range(0, STEPS, part)):
        result[k : k + part] = weighted(scores[i], keys)
        own.append(
            pltpu.make_async_copy(
                result.at[pl.ds(k, part)], out_ref.at[pl.ds(k, part), slot], store_sem.at[EARLY + 4 + i]
            )
        )
        own[-1].start()
    for copy in copies + own:
        copy.wait()


def finish(exchanged):
    dma = pltpu.SemaphoreType.DMA
    return pl.pallas_call(
        finish_kernel,
        out_shape=(
            like(STEPS, SLOTS, HEADS, LATENT), like(SLOTS, ROWS, LATENT), like(SLOTS, ROPE, ROWS),
        ),
        in_specs=[VMEM] * 2 + [ANY] * 3 + [VMEM] * 5,
        out_specs=(HBM,) * 3,
        scratch_shapes=[
            buffer(STEPS, HEADS, LATENT), buffer(ROWS, LATENT), buffer(ROPE, ROWS), dma((EARLY + 6,)),
        ],
        compiler_params=pltpu.CompilerParams(vmem_limit_bytes=20 * 2**20),
        cost_estimate=pl.CostEstimate(
            flops=900_000_000, bytes_accessed=12 * 2**20, transcendentals=400_000
        ),
        name="finish",
    )(*exchanged)


def body(latent_cache, rope_cache, q_latent, q_rope, new_latent, new_rope, req_length, req_dest):
    in_hbm = lambda array: pltpu.with_memory_space_constraint(array, pltpu.HBM)
    latent_cache, rope_cache, req_dest, req_length = map(in_hbm, (latent_cache, rope_cache, req_dest, req_length))
    queries = tuple(map(in_hbm, (q_latent, q_rope, new_latent, new_rope)))
    exchanged = exchange(req_dest, req_length, latent_cache, rope_cache, *queries)
    return finish(exchanged)


def solution(mesh):
    return jax.shard_map(
        body,
        mesh=mesh,
        in_specs=(
            P(("group", "dp"), None, None),
            P(("group", "dp"), None, None),
            P(None, ("group", "dp"), None, None),
            P(None, ("group", "dp"), None, None),
            P(None, ("group", "dp"), None),
            P(None, ("group", "dp"), None),
            P("group"),
            P("group"),
        ),
        out_specs=(
            P(None, ("group", "dp"), None, None),
            P(("group", "dp"), None, None),
            P(("group", "dp"), None, None),
        ),
        check_vma=False,
    )
```

```python
import math

import jax
import jax.numpy as jnp
from jax import lax
from jax.experimental import pallas as pl
from jax.experimental.pallas import tpu as pltpu
from jax.sharding import PartitionSpec as P

MESH = pl.DeviceIdType.MESH
RANKS = 32
RING = 8
SLOTS = 4
ROWS = 384
LATENT = 512
ROPE = 64
STEPS = 8
HEADS = 128
PIECE_ROWS = 48
TILE = 128
SENT_ROWS = 368
SHORT_ROWS = 32
ROPE_UNITS = 14
TWICE = 24
EARLY = 3
LOG2E_SCALE = 192.0 ** (-0.5) * math.log2(math.e)


def shifted(rank, k):
    y, z = rank // RING, rank % RING
    return (y + k // RING) % 4 * RING + (z + 3 * k) % RING


def rope_place(rank):
    y, z = rank // RING, rank % RING
    return (y + z) % 2 * 16 + y * 4 + z // 2


def rope_rank(place):
    half, y, z = place // 16, place % 16 // 4, place % 4
    return y * RING + 2 * z + (y + half) % 2


def piece_of(rank, slot):
    return rank if slot % 2 == 0 else rank + 4 - 8 * (rank // 4 % 2)


def latent_piece(ref, slot, piece, rows):
    row = pl.multiple_of(piece // 4 * PIECE_ROWS, PIECE_ROWS)
    column = pl.multiple_of(piece % 4 * TILE, TILE)
    return ref.at[slot, pl.ds(row, rows), pl.ds(column, TILE)]


def by_length(piece, action):
    pl.when(piece // 4 == 7)(lambda: action(SHORT_ROWS))
    pl.when(piece // 4 != 7)(lambda: action(PIECE_ROWS))


def packed(rows):
    wide = rows.astype(jnp.float32)
    return jnp.concatenate([wide[:, k * TILE : (k + 1) * TILE] for k in range(4)], axis=0).astype(jnp.bfloat16)


def unpacked(latent, units):
    wide = units.astype(jnp.float32)
    rows = jnp.concatenate([wide[8 * k : 8 * k + 8] for k in range(4)], axis=1)
    rows = jnp.concatenate([rows, jnp.zeros_like(rows)], axis=0).astype(jnp.bfloat16)
    return jnp.concatenate([latent, rows], axis=0)


def rope_unit(ref, slot, unit):
    row = pl.multiple_of(unit % 4 * 16, 16)
    column = pl.multiple_of(unit // 4 * TILE, TILE)
    return ref.at[slot, pl.ds(row, 16), pl.ds(column, TILE)]


def placed_new(length, fresh, fresh_rope):
    row = lax.broadcasted_iota(jnp.int32, (ROWS, STEPS), 0)
    step = lax.broadcasted_iota(jnp.int32, (ROWS, STEPS), 1)
    placed = jnp.where(row - length == step, 1.0, 0.0).astype(jnp.bfloat16)
    added = jnp.dot(placed, fresh, preferred_element_type=jnp.float32)
    added_rope = lax.dot_general(
        fresh_rope, placed, (((0,), (1,)), ((), ())), preferred_element_type=jnp.float32
    )
    return added.astype(jnp.bfloat16), added_rope.astype(jnp.bfloat16)


def merged(length, latent, rope, added, added_rope):
    position = lax.broadcasted_iota(jnp.int32, (ROWS, LATENT), 0)
    position_rope = lax.broadcasted_iota(jnp.int32, (ROPE, ROWS), 1)
    return (
        jnp.where(position < length, latent, added),
        jnp.where(position_rope < length, rope, added_rope),
    )


def turned(q_rope):
    return jnp.concatenate([q_rope[t].T for t in range(STEPS)], axis=0)


def scores_of(length, keys_ref, keys_rope_ref, q, q_rope, first=0):
    steps = q.shape[0]
    shape = (steps * HEADS, ROWS)
    step = first + lax.broadcasted_iota(jnp.int32, shape, 0) // HEADS
    seen = lax.broadcasted_iota(jnp.int32, shape, 1) - step <= length
    scores = lax.dot_general(
        q.reshape(steps * HEADS, LATENT), keys_ref[...], (((1,), (1,)), ((), ())),
        preferred_element_type=jnp.float32,
    ) + jnp.dot(q_rope, keys_rope_ref[...], preferred_element_type=jnp.float32)
    return jnp.where(seen, scores * LOG2E_SCALE, -jnp.inf)


def weighted(scores, keys_ref):
    raised = jnp.exp2(scores - jnp.max(scores, axis=1, keepdims=True))
    total = jnp.sum(raised, axis=1, keepdims=True)
    result = jnp.dot(raised.astype(jnp.bfloat16), keys_ref[...], preferred_element_type=jnp.float32)
    return (result * (1.0 / total)).astype(jnp.bfloat16).reshape(-1, HEADS, LATENT)


def attention_of(length, keys_ref, keys_rope_ref, q, q_rope):
    return weighted(scores_of(length, keys_ref, keys_rope_ref, q, q_rope), keys_ref)


def exchange_kernel(
    dest_hbm, length_hbm, latent_ref, rope_ref, q_ref, q_rope_ref, new_hbm, new_rope_hbm,
    out_latent, out_rope, out_early, out_moved, out_moved_rope, out_q, out_q_rope,
    out_added, out_added_rope, out_length,
    held, staged, held_rope, staged_rope,
    q_early, q_rope_all, q_turned, arrived, arrived_rope, early, moved, moved_rope,
    send_one, recv_one, send_two, recv_two,
    send_one_rope, recv_one_rope, send_two_rope, recv_two_rope,
    load_sem, store_sem, dest_ref, length_ref, new_ref, new_rope_ref, added, added_rope, length_row, small_sem,
    units, tail, send_one_short,
):
    me = lax.axis_index("dp")
    place = rope_place(me)
    barrier = pltpu.get_barrier_semaphore()

    @pl.loop(1, RANKS)
    def _(k):
        pl.semaphore_signal(barrier, inc=1, device_id={"dp": shifted(me, k)}, device_id_type=MESH)

    small = [
        pltpu.make_async_copy(source, target, small_sem.at[i])
        for i, (source, target) in enumerate(
            ((dest_hbm, dest_ref), (length_hbm, length_ref), (new_hbm, new_ref), (new_rope_hbm, new_rope_ref))
        )
    ]
    for copy in small:
        copy.start()
    load_units = pltpu.make_async_copy(rope_ref, units.at[:, :, pl.ds(0, ROWS)], small_sem.at[4])
    load_tail = pltpu.make_async_copy(latent_ref.at[:, pl.ds(SENT_ROWS, 16)], tail, small_sem.at[5])
    load_units.start()
    load_tail.start()
    pl.semaphore_wait(barrier, RANKS - 1)

    def send_rope(slot):
        @pl.loop(0, ROPE_UNITS)
        def _(i):
            q = (i + me) % ROPE_UNITS
            unit = slot * ROPE_UNITS + q
            peer, u = rope_rank(unit % RANKS), unit // RANKS
            source = rope_unit(units, slot, q)

            for w in range(2):
                if slot * ROPE_UNITS // RANKS <= w <= (slot * ROPE_UNITS + ROPE_UNITS - 1) // RANKS:
                    target = held_rope[w].at[me]

                    @pl.when((u == w) & (peer == me))
                    def _():
                        pltpu.make_async_copy(source, target, recv_one_rope.at[w]).start()

                    @pl.when((u == w) & (peer != me))
                    def _():
                        pltpu.make_async_remote_copy(
                            source, target, send_one_rope.at[slot], recv_one_rope.at[w],
                            device_id={"dp": peer}, device_id_type=MESH,
                        ).start()

    for slot in range(SLOTS):
        if slot == 0:
            load_units.wait()
            load_tail.wait()
            for k in range(SLOTS):
                units[k, 0:32, ROWS : ROWS + TILE] = packed(tail[k, 0:8, :])
        send_rope(slot)

        def keep(rows):
            pltpu.make_async_copy(
                latent_piece(latent_ref, slot, piece_of(me, slot), rows),
                held[slot].at[me, pl.ds(0, rows)], recv_one.at[slot],
            ).start()

        by_length(piece_of(me, slot), keep)

        @pl.loop(1, RANKS)
        def _(k):
            peer = shifted(me, k)
            piece = piece_of(peer, slot)

            def send(rows):
                pltpu.make_async_remote_copy(
                    latent_piece(latent_ref, slot, piece, rows), held[slot].at[me, pl.ds(0, rows)],
                    (send_one_short if rows == SHORT_ROWS else send_one).at[slot], recv_one.at[slot],
                    device_id={"dp": peer}, device_id_type=MESH,
                ).start()

            by_length(piece, send)

    load_q = pltpu.make_async_copy(q_ref.at[:, pl.ds(0, EARLY)], q_early, load_sem.at[0])
    load_q_rope = pltpu.make_async_copy(q_rope_ref, q_rope_all, load_sem.at[1])
    load_last = pltpu.make_async_copy(q_ref.at[:, EARLY], out_q, load_sem.at[4])
    load_last.start()
    load_q.start()
    load_q_rope.start()

    def forward_rope(u):
        pltpu.make_async_copy(held_rope[u], held_rope[u], recv_one_rope.at[u]).wait()
        unit = place + RANKS * u
        slot, q = unit // ROPE_UNITS, unit % ROPE_UNITS

        @pl.loop(0, RANKS)
        def _(k):
            peer = shifted(me, k)
            origin = dest_ref[peer * SLOTS + slot]
            staged_rope[u, peer] = held_rope[u][origin]
            source, target = staged_rope.at[u, peer], rope_unit(out_rope, slot, q)

            @pl.when(k == 0)
            def _():
                pltpu.make_async_copy(source, target, recv_two_rope.at[slot]).start()

            @pl.when(k != 0)
            def _():
                pltpu.make_async_remote_copy(
                    source, target, send_two_rope.at[u], recv_two_rope.at[slot],
                    device_id={"dp": peer}, device_id_type=MESH,
                ).start()

    for copy in small:
        copy.wait()
    for slot in range(SLOTS):
        for u in range(2):
            first, last = slot * ROPE_UNITS - RANKS * u, slot * ROPE_UNITS + ROPE_UNITS - RANKS * u
            first, last = max(first, 0), min(last, RANKS if u == 0 else TWICE)
            if first < last:
                pl.when((place >= first) & (place < last))(lambda u=u: forward_rope(u))

        mine = piece_of(me, slot)

        def forward(rows):
            part = held[slot].at[:, pl.ds(0, rows)]
            pltpu.make_async_copy(part, part, recv_one.at[slot]).wait()

            @pl.loop(0, RANKS)
            def _(k):
                peer = shifted(me, k)
                origin = dest_ref[peer * SLOTS + slot]
                staged[slot, peer, 0:rows] = held[slot][origin, 0:rows]
                source = staged.at[slot, peer, pl.ds(0, rows)]
                target = latent_piece(out_latent, slot, mine, rows)

                @pl.when(k == 0)
                def _():
                    pltpu.make_async_copy(source, target, recv_two.at[slot]).start()

                @pl.when(k != 0)
                def _():
                    pltpu.make_async_remote_copy(
                        source, target, send_two.at[slot], recv_two.at[slot],
                        device_id={"dp": peer}, device_id_type=MESH,
                    ).start()

        by_length(mine, forward)

    def arrive(slot):
        rows = out_latent.at[slot, pl.ds(0, SENT_ROWS)]
        pltpu.make_async_copy(rows, rows, recv_two.at[slot]).wait()
        part = staged_rope.at[0, pl.ds(0, ROPE_UNITS)]
        pltpu.make_async_copy(part, part, recv_two_rope.at[slot]).wait()

    def stores(slot):
        return [
            pltpu.make_async_copy(early.at[slot], out_early.at[slot], store_sem.at[0, slot]),
            pltpu.make_async_copy(moved.at[slot], out_moved.at[slot], store_sem.at[1, slot]),
            pltpu.make_async_copy(moved_rope.at[slot], out_moved_rope.at[slot], store_sem.at[2, slot]),
        ]

    load_q.wait()
    load_q_rope.wait()
    q_turned[...] = turned(q_rope_all[:, EARLY])
    store_turned = pltpu.make_async_copy(q_turned, out_q_rope, load_sem.at[5])
    store_turned.start()
    last_length = length_ref[dest_ref[me * SLOTS + EARLY] * SLOTS + EARLY]
    added[...], added_rope[...] = placed_new(last_length, new_ref[:, EARLY, :], new_rope_ref[:, EARLY, :])
    length_row[...] = jnp.full((8, TILE), last_length, jnp.int32)
    last = [
        pltpu.make_async_copy(added, out_added, load_sem.at[6]),
        pltpu.make_async_copy(added_rope, out_added_rope, load_sem.at[7]),
        pltpu.make_async_copy(length_row, out_length, load_sem.at[8]),
    ]
    for copy in last:
        copy.start()
    for slot in range(EARLY):
        arrive(slot)
        load = pltpu.make_async_copy(out_latent.at[slot, pl.ds(0, SENT_ROWS)], arrived, load_sem.at[2])
        load_rope = pltpu.make_async_copy(out_rope.at[slot], arrived_rope, load_sem.at[3])
        load.start()
        load_rope.start()
        load.wait()
        load_rope.wait()
        length = length_ref[dest_ref[me * SLOTS + slot] * SLOTS + slot]
        moved[slot], moved_rope[slot] = merged(
            length, unpacked(arrived[...], arrived_rope[0:32, ROWS:]), arrived_rope[:, :ROWS],
            *placed_new(length, new_ref[:, slot, :], new_rope_ref[:, slot, :]),
        )
        early[slot] = attention_of(
            length, moved.at[slot], moved_rope.at[slot], q_early[:, slot], turned(q_rope_all[:, slot])
        )
        for copy in stores(slot):
            copy.start()

    others = pl.ds(0, RANKS - 1)
    for slot in range(SLOTS):
        def sent(rows):
            short = 3 if rows == SHORT_ROWS else 4
            part = held[slot].at[pl.ds(0, RANKS - 1 - short)]
            pltpu.make_async_copy(part, part, send_one.at[slot]).wait()
            part = held[slot].at[pl.ds(0, short), pl.ds(0, SHORT_ROWS)]
            pltpu.make_async_copy(part, part, send_one_short.at[slot]).wait()

        by_length(piece_of(me, slot), sent)
        own = place // ROPE_UNITS == slot
        own |= (place < TWICE) & ((place + RANKS) // ROPE_UNITS == slot)

        @pl.when(own)
        def _():
            part = held_rope[0].at[pl.ds(0, ROPE_UNITS - 1)]
            pltpu.make_async_copy(part, part, send_one_rope.at[slot]).wait()

        @pl.when(jnp.logical_not(own))
        def _():
            part = held_rope[0].at[pl.ds(0, ROPE_UNITS)]
            pltpu.make_async_copy(part, part, send_one_rope.at[slot]).wait()

    load_last.wait()
    store_turned.wait()
    for copy in last:
        copy.wait()
    for slot in range(EARLY):
        for copy in stores(slot):
            copy.wait()
    for slot in range(SLOTS):
        def sent(rows):
            part = staged.at[slot, others, pl.ds(0, rows)]
            pltpu.make_async_copy(part, part, send_two.at[slot]).wait()

        by_length(piece_of(me, slot), sent)

    rest = staged_rope.at[0, others]
    pltpu.make_async_copy(rest, rest, send_two_rope.at[0]).wait()

    @pl.when(place < TWICE)
    def _():
        pltpu.make_async_copy(rest, rest, send_two_rope.at[1]).wait()

    for slot in range(EARLY, SLOTS):
        arrive(slot)


HBM = pl.BlockSpec(memory_space=pltpu.HBM)
ANY = pl.BlockSpec(memory_space=pl.ANY)
VMEM = pl.BlockSpec(memory_space=pltpu.VMEM)


def like(*shape):
    return jax.ShapeDtypeStruct(shape, jnp.bfloat16)


def buffer(*shape):
    return pltpu.VMEM(shape, jnp.bfloat16)


def exchange(req_dest, req_length, latent_cache, rope_cache, q_latent, q_rope, new_latent, new_rope):
    dma = pltpu.SemaphoreType.DMA
    return pl.pallas_call(
        exchange_kernel,
        out_shape=(
            buffer(SLOTS, ROWS, LATENT), buffer(SLOTS, ROPE, ROWS + TILE),
            buffer(EARLY, STEPS, HEADS, LATENT), buffer(EARLY, ROWS, LATENT), buffer(EARLY, ROPE, ROWS),
            buffer(STEPS, HEADS, LATENT), buffer(STEPS * HEADS, ROPE),
            buffer(ROWS, LATENT), buffer(ROPE, ROWS), pltpu.VMEM((8, TILE), jnp.int32),
        ),
        in_specs=[HBM] * 8,
        out_specs=(ANY,) * 10,
        scratch_shapes=[
            (buffer(RANKS, PIECE_ROWS, TILE),) * SLOTS,
            buffer(SLOTS, RANKS, PIECE_ROWS, TILE),
            (buffer(RANKS, 16, TILE),) * 2,
            buffer(2, RANKS, 16, TILE),
            buffer(STEPS, EARLY, HEADS, LATENT), buffer(STEPS, SLOTS, ROPE, HEADS),
            buffer(STEPS * HEADS, ROPE),
            buffer(SENT_ROWS, LATENT), buffer(ROPE, ROWS + TILE),
            buffer(EARLY, STEPS, HEADS, LATENT), buffer(EARLY, ROWS, LATENT), buffer(EARLY, ROPE, ROWS),
            dma((SLOTS,)), dma((SLOTS,)), dma((SLOTS,)), dma((SLOTS,)),
            dma((SLOTS,)), dma((2,)), dma((2,)), dma((SLOTS,)),
            dma((9,)), dma((3, EARLY)),
            pltpu.SMEM(req_dest.shape, jnp.int32), pltpu.SMEM(req_length.shape, jnp.int32),
            buffer(*new_latent.shape), buffer(*new_rope.shape),
            buffer(ROWS, LATENT), buffer(ROPE, ROWS), pltpu.VMEM((8, TILE), jnp.int32), dma((6,)),
            buffer(SLOTS, ROPE, ROWS + TILE), buffer(SLOTS, 16, LATENT), dma((SLOTS,)),
        ],
        compiler_params=pltpu.CompilerParams(
            collective_id=0, has_side_effects=True, vmem_limit_bytes=32 * 2**20
        ),
        cost_estimate=pl.CostEstimate(
            flops=2_600_000_000, bytes_accessed=16 * 2**20, transcendentals=1_200_000
        ),
        name="exchange",
    )(req_dest, req_length, latent_cache, rope_cache, q_latent, q_rope, new_latent, new_rope)


def finish_kernel(
    latent_ref, rope_ref, early_ref, moved_ref, moved_rope_ref, q, q_rope, added, added_rope, length_ref,
    out_ref, out_moved, out_moved_rope,
    result, keys, keys_rope, store_sem,
):
    slot = EARLY
    copies = [
        pltpu.make_async_copy(early_ref.at[k], out_ref.at[:, k], store_sem.at[k]) for k in range(EARLY)
    ] + [
        pltpu.make_async_copy(moved_ref, out_moved.at[pl.ds(0, EARLY)], store_sem.at[EARLY]),
        pltpu.make_async_copy(moved_rope_ref, out_moved_rope.at[pl.ds(0, EARLY)], store_sem.at[EARLY + 1]),
    ]
    for copy in copies:
        copy.start()
    length = length_ref[:1, :1]
    keys[...], keys_rope[...] = merged(
        length, unpacked(latent_ref[slot, :SENT_ROWS], rope_ref[slot, 0:32, ROWS:]), rope_ref[slot, :, :ROWS],
        added[...], added_rope[...],
    )
    part = STEPS // 2
    own = [
        pltpu.make_async_copy(keys, out_moved.at[slot], store_sem.at[EARLY + 2]),
        pltpu.make_async_copy(keys_rope, out_moved_rope.at[slot], store_sem.at[EARLY + 3]),
    ]
    own[0].start()
    own[1].start()
    scores = [
        scores_of(length, keys, keys_rope, q[k : k + part], q_rope[k * HEADS : (k + part) * HEADS], k)
        for k in range(0, STEPS, part)
    ]
    for i, k in enumerate(range(0, STEPS, part)):
        result[k : k + part] = weighted(scores[i], keys)
        own.append(
            pltpu.make_async_copy(
                result.at[pl.ds(k, part)], out_ref.at[pl.ds(k, part), slot], store_sem.at[EARLY + 4 + i]
            )
        )
        own[-1].start()
    for copy in copies + own:
        copy.wait()


def finish(exchanged):
    dma = pltpu.SemaphoreType.DMA
    return pl.pallas_call(
        finish_kernel,
        out_shape=(
            like(STEPS, SLOTS, HEADS, LATENT), like(SLOTS, ROWS, LATENT), like(SLOTS, ROPE, ROWS),
        ),
        in_specs=[VMEM] * 2 + [ANY] * 3 + [VMEM] * 5,
        out_specs=(HBM,) * 3,
        scratch_shapes=[
            buffer(STEPS, HEADS, LATENT), buffer(ROWS, LATENT), buffer(ROPE, ROWS), dma((EARLY + 6,)),
        ],
        compiler_params=pltpu.CompilerParams(vmem_limit_bytes=20 * 2**20),
        cost_estimate=pl.CostEstimate(
            flops=900_000_000, bytes_accessed=12 * 2**20, transcendentals=400_000
        ),
        name="finish",
    )(*exchanged)


def body(latent_cache, rope_cache, q_latent, q_rope, new_latent, new_rope, req_length, req_dest):
    in_hbm = lambda array: pltpu.with_memory_space_constraint(array, pltpu.HBM)
    latent_cache, rope_cache, req_dest, req_length = map(in_hbm, (latent_cache, rope_cache, req_dest, req_length))
    queries = tuple(map(in_hbm, (q_latent, q_rope, new_latent, new_rope)))
    exchanged = exchange(req_dest, req_length, latent_cache, rope_cache, *queries)
    return finish(exchanged)


def solution(mesh):
    return jax.shard_map(
        body,
        mesh=mesh,
        in_specs=(
            P(("group", "dp"), None, None),
            P(("group", "dp"), None, None),
            P(None, ("group", "dp"), None, None),
            P(None, ("group", "dp"), None, None),
            P(None, ("group", "dp"), None),
            P(None, ("group", "dp"), None),
            P("group"),
            P("group"),
        ),
        out_specs=(
            P(None, ("group", "dp"), None, None),
            P(("group", "dp"), None, None),
            P(("group", "dp"), None, None),
        ),
        check_vma=False,
    )
```
